512 devices in a mesh: loop: 32 (over y_hi, z), group: 16 (over x, y_lo, core).
Axes of the slice: x: 4, y: 8 (y_hi: 4, y_lo: 2; y = y_hi * 2 + y_lo), z: 8, core: 2. Of those that a mesh axis runs over, the one named last changes fastest.
Arguments:
- cand_query: bfloat16 [16, 4096, 2048], P('group', 'loop'), may hold values from -6 to 6
- cand_kv: bfloat16 [16, 4096, 4096], P('group', 'loop'), may hold values from -6 to 6
- cand_gate: bfloat16 [16, 4096, 2048], P('group', 'loop'), may hold values from -6 to 6
- cache_store: bfloat16 [256, 32, 4, 4096], P('group', 'loop'), may hold values from -6 to 6
- holders: int32 [256], replicated, may hold values from 0 to 255, as said below
- lengths: int32 [16], P('group'), may hold values from 256 to 2048, as said below
- buckets: int32 [16, 2048], P('group'), may hold values from 0 to 127
- time_bias: float32 [128, 16], replicated, may hold values from -3 to 3
- self_bias: float32 [16], replicated, may hold values from 2 to 4
- norm_gain: float32 [2048], replicated, may hold values from 0.5 to 1.5
Outputs:
- gated_output: bfloat16 [16, 4096, 2048], P('group', 'loop')
The draws below stay inside these ranges and needn't reach their ends.
Inputs may be any that keep to these rules, and one draw needn't show every extreme that they name: `holders`: entry g * 16 + j names the cache slot of piece j of session g; every slot is named once; slot s lies in group s // 16; every group holds exactly 1 pieces of every session. `lengths`: some session has exactly 2048 positions in every draw.
All inputs are finite; a program needn't handle non-finite values.
Results may differ from the reference program's by a relative error of at most 0.005.
Values may be sent and summed in bfloat16 or wider, within the bound.
No kernel may reach another device: no remote copies, remote signals or barrier semaphores. Data moves between devices by JAX's collectives and lax.ppermute only.
A program may use at most 64 MiB of HBM per device.

```python
import math
import jax
import jax.numpy as jnp
from jax import lax

D = 2048
HEADS = 16
NB = 128
PIECES = 16
HIST_DEV = 64
CAND_DEV = 128
HISTORY = 2048
PIECE_LEN = 4
N_LOOP = 32
N_GROUP = 16


def draw_holders(key, part):
    key = jax.random.fold_in(key, 11)
    group_count = N_GROUP
    slot_count = PIECES
    base = slot_count // group_count
    counts = jnp.full((group_count, group_count), base, jnp.int32)

    def one_holder(count_row, holder_key):
        targets = jnp.repeat(jnp.arange(group_count, dtype=jnp.int32), count_row, total_repeat_length=slot_count)
        return jax.random.permutation(holder_key, targets)
    holder_keys = jax.random.split(jax.random.fold_in(key, 2), group_count)
    slot_target = jax.vmap(one_holder)(counts, holder_keys).reshape(-1)
    tiebreak = jax.random.permutation(jax.random.fold_in(key, 3), group_count * slot_count).astype(jnp.int32)
    sort_key = slot_target * (group_count * slot_count) + tiebreak
    return jnp.argsort(sort_key).astype(jnp.int32)


def draw_lengths(key, part):
    key = jax.random.fold_in(key, 23)
    span_total = N_LOOP * HIST_DEV
    drawn = jax.random.randint(jax.random.fold_in(key, 1), (N_GROUP,), span_total // 8, span_total + 1, dtype=jnp.int32)
    chosen = jax.random.randint(jax.random.fold_in(key, 2), (), 0, N_GROUP, dtype=jnp.int32)
    return jnp.where(jnp.arange(N_GROUP, dtype=jnp.int32) == chosen, span_total, drawn)


def place_ends(entries, own_key, smallest, top_value):
    longest = entries.shape.index(max(entries.shape))
    spots = []
    for shift in (0, 1):
        where = [jax.random.randint(jax.random.fold_in(own_key, axis), (), 0, length) for axis, length in enumerate(entries.shape)]
        where[longest] = (where[longest] + shift) % entries.shape[longest]
        spots.append(tuple(where))
    return entries.at[spots[0]].set(smallest).at[spots[1]].set(top_value)


def block_levels(rng, dims, cuts, smallest, top_value):
    factor_of, own = 1.0, jax.random.fold_in(rng, 6)
    for position, blocks in cuts:
        draws = jnp.exp(jax.random.uniform(jax.random.fold_in(own, position), (blocks,), jnp.float32, smallest / len(cuts), top_value / len(cuts)))
        factor_of = factor_of * jnp.repeat(draws, dims[position] // blocks).reshape([-1 if axis == position else 1 for axis in range(len(dims))])
    return factor_of


def gaussian(key, shape, scale, limit, cuts=(), held_as=jnp.bfloat16):
    level = block_levels(key, shape, cuts, -0.22, 0.18) if cuts else 1.0
    entries = jax.random.normal(key, shape, jnp.float32) * scale * level
    return jnp.minimum(jnp.maximum(entries, -limit), limit).astype(held_as)


def setup_inputs(seed: int = 0) -> dict:
    key_of = jax.random.split(jax.random.key(seed), 11)
    cand_query = gaussian(key_of[0], (N_GROUP, N_LOOP * CAND_DEV, D), 1.0, 6.0, ((0, 16), (1, 32)))
    cand_kv = gaussian(key_of[1], (N_GROUP, N_LOOP * CAND_DEV, 2 * D), 1.0, 6.0, ((0, 16), (1, 32)))
    cand_gate = gaussian(key_of[2], (N_GROUP, N_LOOP * CAND_DEV, D), 1.0, 6.0, ((0, 16), (1, 32)))
    cache_store = gaussian(key_of[3], (N_GROUP * PIECES, N_LOOP, PIECE_LEN, 2 * D), 1.0, 6.0, ((0, 16), (1, 32)))
    holders = draw_holders(jax.random.fold_in(key_of[10], 71), 0)
    lengths = draw_lengths(jax.random.fold_in(key_of[10], 71), 0)
    buckets = place_ends(jax.random.randint(key_of[6], (N_GROUP, HISTORY), 0, NB), jax.random.fold_in(key_of[6], 1), 0, NB - 1).astype(jnp.int32)
    time_bias = gaussian(key_of[7], (NB, HEADS), 0.5, 3.0, (), jnp.float32)
    self_bias = jnp.clip(jax.random.uniform(key_of[8], (HEADS,), jnp.float32, 2.0, 4.0), 2.0, 4.0)
    norm_gain = jnp.clip(1.0 + 0.1 * jax.random.normal(key_of[9], (D,), jnp.float32), 0.5, 1.5)
    return {"cand_query": cand_query, "cand_kv": cand_kv, "cand_gate": cand_gate, "cache_store": cache_store, "holders": holders, "lengths": lengths, "buckets": buckets, "time_bias": time_bias, "self_bias": self_bias, "norm_gain": norm_gain}


def reference(cand_query, cand_kv, cand_gate, cache_store, holders, lengths, buckets, time_bias, self_bias, norm_gain):
    head_dim = D // HEADS
    scaling = 1.0 / math.sqrt(head_dim)
    span_total = N_LOOP * HIST_DEV

    def one_group(group_index):
        slot_ids = lax.dynamic_slice_in_dim(holders, (group_index * PIECES).astype(jnp.int32), PIECES)
        pieces = cache_store[slot_ids]
        history = jnp.transpose(pieces, (1, 0, 2, 3)).reshape(span_total, 2 * D).astype(jnp.float32)
        key_heads = history[:, :D].reshape(span_total, HEADS, head_dim)
        value_heads = history[:, D:].reshape(span_total, HEADS, head_dim)
        time_term = jnp.transpose(time_bias[buckets[group_index]], (1, 0))
        in_range = jnp.arange(span_total, dtype=jnp.int32) < lengths[group_index]
        queries = cand_query[group_index]
        pairs = cand_kv[group_index]
        gates = cand_gate[group_index]

        def one_block(block_index):
            first_row = (block_index * CAND_DEV).astype(jnp.int32)
            block_queries = lax.dynamic_slice_in_dim(queries, first_row, CAND_DEV).astype(jnp.float32).reshape(CAND_DEV, HEADS, head_dim)
            own_pairs = lax.dynamic_slice_in_dim(pairs, first_row, CAND_DEV).astype(jnp.float32)
            gate_rows = lax.dynamic_slice_in_dim(gates, first_row, CAND_DEV).astype(jnp.float32)
            scores = jnp.einsum('chd,khd->hck', block_queries, key_heads, precision=lax.Precision.HIGHEST) * scaling
            scores = scores + time_term[:, None, :]
            weights = jnp.where(in_range[None, None, :], jax.nn.silu(scores), 0.0).astype(jnp.bfloat16)
            weights = lax.optimization_barrier(weights).astype(jnp.float32)
            attended = jnp.einsum('hck,khd->chd', weights, value_heads, precision=lax.Precision.HIGHEST)
            own_keys = own_pairs[:, :D].reshape(CAND_DEV, HEADS, head_dim)
            own_values = own_pairs[:, D:].reshape(CAND_DEV, HEADS, head_dim)
            own_scores = lax.optimization_barrier(jnp.sum(block_queries * own_keys, axis=2)) * scaling + self_bias
            own_weights = jax.nn.silu(own_scores).astype(jnp.bfloat16)
            own_weights = lax.optimization_barrier(own_weights).astype(jnp.float32)
            attended = (attended + own_weights[:, :, None] * own_values).reshape(CAND_DEV, D)
            average = lax.optimization_barrier(jnp.mean(attended, axis=-1, keepdims=True))
            centered = attended - average
            variance = lax.optimization_barrier(jnp.mean(centered * centered, axis=-1, keepdims=True))
            normed = centered * lax.rsqrt(variance + 1e-05) * norm_gain * gate_rows
            return normed.astype(jnp.bfloat16)
        blocks = lax.map(one_block, jnp.arange(N_LOOP, dtype=jnp.int32))
        return blocks.reshape(N_LOOP * CAND_DEV, D)
    return lax.map(one_group, jnp.arange(N_GROUP, dtype=jnp.int32))
```

```python
import math

import jax
import jax.numpy as jnp
from jax import lax
from jax.experimental import pallas as pl
from jax.experimental.pallas import tpu as pltpu
from jax.sharding import Mesh
from jax.sharding import PartitionSpec as P

HEADS = 16
HEAD_DIM = 128
GROUP = ("x", "ylo", "core")
LOOP = ("yhi", "z")


def shifted(value, axis, steps):
    count = lax.axis_size(axis)
    return lax.ppermute(value, axis, [(i, (i + steps) % count) for i in range(count)])


def gathered(value, axis):
    count = lax.axis_size(axis)
    index = lax.axis_index(axis)
    parts = [value] + [shifted(value, axis, s) for s in range(1, count)]
    stacked = jnp.stack(parts)
    order = (index - jnp.arange(count)) % count
    return stacked[order]


def attend_kernel(q_ref, k_ref, v_ref, bias_ref, valid_ref, out_ref):
    scale = 0.5 / math.sqrt(HEAD_DIM)
    keys = k_ref[...]
    values = v_ref[...] * valid_ref[...]
    bias = bias_ref[0] * 0.5
    for block in range(q_ref.shape[0]):
        scores = lax.dot_general(
            q_ref[block], keys, (((1,), (1,)), ((), ())), preferred_element_type=jnp.float32
        )
        half = scores * scale + bias
        weights = (half + half * jnp.tanh(half)).astype(jnp.bfloat16)
        out_ref[block] = jnp.dot(
            weights, values, preferred_element_type=jnp.float32
        ).astype(out_ref.dtype)


def attend(queries, history, bias, valid):
    blocks, rows, width = queries.shape
    positions = history.shape[0]
    heads = width // HEAD_DIM
    return pl.pallas_call(
        attend_kernel,
        grid=(heads,),
        in_specs=[
            pl.BlockSpec((blocks, rows, HEAD_DIM), lambda h: (0, 0, h)),
            pl.BlockSpec((positions, HEAD_DIM), lambda h: (0, h)),
            pl.BlockSpec((positions, HEAD_DIM), lambda h: (0, h + heads)),
            pl.BlockSpec((1, 1, positions), lambda h: (h, 0, 0)),
            pl.BlockSpec((positions, HEAD_DIM), lambda h: (0, 0)),
        ],
        out_specs=pl.BlockSpec((blocks, rows, HEAD_DIM), lambda h: (0, 0, h)),
        out_shape=jax.ShapeDtypeStruct((blocks, rows, width), jnp.bfloat16),
        compiler_params=pltpu.CompilerParams(vmem_limit_bytes=32 * 1024 * 1024),
        cost_estimate=pl.CostEstimate(
            flops=4 * blocks * rows * positions * width,
            bytes_accessed=4 * blocks * rows * width + 4 * positions * width,
            transcendentals=blocks * rows * positions * heads,
        ),
    )(queries, history, history, bias, valid)


def finish_kernel(part_ref, q_ref, own_ref, gate_ref, self_bias_ref, gain_ref, out_ref):
    width = q_ref.shape[1]
    scale = 0.5 / math.sqrt(HEAD_DIM)
    pieces = []
    for head in range(width // HEAD_DIM):
        cols = slice(head * HEAD_DIM, (head + 1) * HEAD_DIM)
        value_cols = slice(width + head * HEAD_DIM, width + (head + 1) * HEAD_DIM)
        product = q_ref[:, cols].astype(jnp.float32) * own_ref[:, cols].astype(jnp.float32)
        half = jnp.sum(product, axis=-1, keepdims=True) * scale + 0.5 * self_bias_ref[0, head]
        weight = (half + half * jnp.tanh(half)).astype(jnp.bfloat16).astype(jnp.float32)
        pieces.append(
            part_ref[:, cols].astype(jnp.float32)
            + weight * own_ref[:, value_cols].astype(jnp.float32)
        )
    total = jnp.concatenate(pieces, axis=-1)
    average = jnp.mean(total, axis=-1, keepdims=True)
    centered = total - average
    variance = jnp.mean(centered * centered, axis=-1, keepdims=True)
    normed = centered * lax.rsqrt(variance + 1e-05) * gain_ref[...]
    out_ref[...] = (normed * gate_ref[...].astype(jnp.float32)).astype(out_ref.dtype)


def finish(partial, queries, own, gate, self_bias, gain):
    rows, width = queries.shape
    block = 32
    row_spec = lambda cols: pl.BlockSpec((block, cols), lambda i: (i, 0))
    return pl.pallas_call(
        finish_kernel,
        grid=(rows // block,),
        in_specs=[
            row_spec(width),
            row_spec(width),
            row_spec(2 * width),
            row_spec(width),
            pl.BlockSpec(memory_space=pltpu.SMEM),
            pl.BlockSpec((1, width), lambda i: (0, 0)),
        ],
        out_specs=row_spec(width),
        out_shape=jax.ShapeDtypeStruct((rows, width), jnp.bfloat16),
        compiler_params=pltpu.CompilerParams(vmem_limit_bytes=32 * 1024 * 1024),
    )(partial, queries, own, gate, self_bias[None], gain[None])


def per_device(
    cand_query,
    cand_kv,
    cand_gate,
    cache_store,
    holders,
    lengths,
    buckets,
    time_bias,
    self_bias,
    norm_gain,
):
    group_index = lax.axis_index(GROUP)
    y_index = lax.axis_index("yhi")
    y_size = lax.axis_size("yhi")
    z_size = lax.axis_size("z")
    groups = lax.axis_size(GROUP)
    slots, _, piece_len, double_width = cache_store.shape
    holding = (holders // slots).reshape(groups, slots)
    slot_of = (holders % slots).reshape(groups, slots)
    mine = holding == group_index
    chosen = jnp.sum(jnp.where(mine, slot_of, 0), axis=1)
    outgoing = cache_store[chosen, 0]
    incoming = lax.all_to_all(outgoing, GROUP, 0, 0, tiled=True)
    pieces = incoming.reshape(slots * piece_len, double_width)
    history = lax.all_gather(pieces, "z", tiled=True)

    own_holding = lax.dynamic_index_in_dim(holding, group_index, 0, keepdims=False)
    arrived = own_holding[None, :] == jnp.arange(groups, dtype=jnp.int32)[:, None]
    piece_of = jnp.sum(jnp.where(arrived, jnp.arange(slots, dtype=jnp.int32)[None, :], 0), axis=1)
    per_y = z_size * slots * piece_len
    bucket_rows = lax.dynamic_slice_in_dim(buckets[0], y_index * per_y, per_y)
    bucket_rows = bucket_rows.reshape(z_size, slots, piece_len)[:, piece_of].reshape(per_y)
    place = (
        y_index * per_y
        + (jnp.arange(z_size, dtype=jnp.int32) * slots * piece_len)[:, None, None]
        + (piece_of * piece_len)[None, :, None]
        + jnp.arange(piece_len, dtype=jnp.int32)[None, None, :]
    ).reshape(per_y)
    one_hot = (
        bucket_rows[:, None] == jnp.arange(time_bias.shape[0], dtype=jnp.int32)[None, :]
    ).astype(jnp.float32)
    bias = jnp.einsum("kn,nh->hk", one_hot, time_bias, precision=lax.Precision.HIGHEST)
    valid = jnp.broadcast_to(
        (place < lengths[0]).astype(jnp.bfloat16)[:, None], (per_y, HEAD_DIM)
    )

    queries = cand_query[0]
    all_queries = gathered(queries, "yhi")
    partial = attend(all_queries, history, bias[:, None, :], valid)
    summed = lax.psum_scatter(partial, "yhi", scatter_dimension=0, tiled=False)
    return finish(summed, queries, cand_kv[0], cand_gate[0], self_bias, norm_gain)[None]


def solution(mesh):
    split = Mesh(mesh.devices.reshape(4, 8, 4, 2, 2), LOOP + GROUP)
    rows = P(GROUP, LOOP, None)
    return jax.shard_map(
        per_device,
        mesh=split,
        in_specs=(
            rows,
            rows,
            rows,
            P(GROUP, LOOP, None, None),
            P(),
            P(GROUP),
            P(GROUP, None),
            P(),
            P(),
            P(),
        ),
        out_specs=rows,
        check_vma=False,
    )
```

```python
import math

import jax
import jax.numpy as jnp
from jax import lax
from jax.experimental import pallas as pl
from jax.experimental.pallas import tpu as pltpu
from jax.sharding import Mesh
from jax.sharding import PartitionSpec as P

HEADS = 16
HEAD_DIM = 128
GROUP = ("x", "ylo", "core")
LOOP = ("yhi", "z")


def shifted(value, axis, steps):
    count = lax.axis_size(axis)
    return lax.ppermute(value, axis, [(i, (i + steps) % count) for i in range(count)])


def make_attend_kernel(count, with_base):
    def kernel(*refs):
        q_refs = refs[:count]
        k_ref, v_ref, bias_ref, valid_ref = refs[count : count + 4]
        base_ref = refs[count + 4] if with_base else None
        out_refs = refs[count + 4 + with_base :]
        rows = q_refs[0].shape[0]
        scale = 0.5 / math.sqrt(HEAD_DIM)
        valid = valid_ref[...]
        for head in range(k_ref.shape[1] // HEAD_DIM):
            cols = slice(head * HEAD_DIM, (head + 1) * HEAD_DIM)
            queries = jnp.concatenate([q_ref[:, cols] for q_ref in q_refs], axis=0)
            scores = lax.dot_general(
                queries,
                k_ref[:, cols],
                (((1,), (1,)), ((), ())),
                preferred_element_type=jnp.float32,
            )
            half = scores * scale + bias_ref[head] * 0.5
            weights = (half + half * jnp.tanh(half)).astype(jnp.bfloat16)
            sums = jnp.dot(weights, v_ref[:, cols] * valid, preferred_element_type=jnp.float32)
            for i, out_ref in enumerate(out_refs):
                block = sums[i * rows : (i + 1) * rows]
                if with_base:
                    block = block + base_ref[:, cols]
                out_ref[:, cols] = block.astype(out_ref.dtype)

    return kernel


def attend(queries, history, bias, valid, types, first, heads, per_step, base=None):
    rows = queries[0].shape[0]
    positions = history.shape[0]
    width = per_step * HEAD_DIM
    steps = heads // per_step
    skip = first // per_step
    all_steps = HEADS // per_step
    count = len(queries)
    out_spec = pl.BlockSpec((rows, width), lambda i: (0, i))
    return pl.pallas_call(
        make_attend_kernel(count, base is not None),
        grid=(steps,),
        in_specs=[pl.BlockSpec((rows, width), lambda i: (0, i + skip))] * count
        + [
            pl.BlockSpec((positions, width), lambda i: (0, i + skip)),
            pl.BlockSpec((positions, width), lambda i: (0, i + skip + all_steps)),
            pl.BlockSpec((per_step, 1, positions), lambda i: (i + skip, 0, 0)),
            pl.BlockSpec((positions, HEAD_DIM), lambda i: (0, 0)),
        ]
        + ([] if base is None else [out_spec]),
        out_specs=[out_spec] * count,
        out_shape=[jax.ShapeDtypeStruct((rows, heads * HEAD_DIM), t) for t in types],
        compiler_params=pltpu.CompilerParams(vmem_limit_bytes=60 * 1024 * 1024),
        cost_estimate=pl.CostEstimate(
            flops=4 * count * rows * positions * heads * HEAD_DIM,
            bytes_accessed=4 * positions * heads * HEAD_DIM,
            transcendentals=count * rows * positions * heads,
        ),
    )(*queries, history, history, bias, valid, *([] if base is None else [base]))


def own_kernel(q_ref, own_ref, self_bias_ref, out_ref):
    width = q_ref.shape[1]
    scale = 0.5 / math.sqrt(HEAD_DIM)
    for head in range(width // HEAD_DIM):
        cols = slice(head * HEAD_DIM, (head + 1) * HEAD_DIM)
        value_cols = slice(width + head * HEAD_DIM, width + (head + 1) * HEAD_DIM)
        product = q_ref[:, cols].astype(jnp.float32) * own_ref[:, cols].astype(jnp.float32)
        half = jnp.sum(product, axis=-1, keepdims=True) * scale + 0.5 * self_bias_ref[0, head]
        weight = (half + half * jnp.tanh(half)).astype(jnp.bfloat16).astype(jnp.float32)
        out_ref[:, cols] = weight * own_ref[:, value_cols].astype(jnp.float32)


def own_term(queries, own, self_bias):
    rows, width = queries.shape
    block = 32
    return pl.pallas_call(
        own_kernel,
        grid=(rows // block,),
        in_specs=[
            pl.BlockSpec((block, width), lambda i: (i, 0)),
            pl.BlockSpec((block, 2 * width), lambda i: (i, 0)),
            pl.BlockSpec(memory_space=pltpu.SMEM),
        ],
        out_specs=pl.BlockSpec((block, width), lambda i: (i, 0)),
        out_shape=jax.ShapeDtypeStruct((rows, width), jnp.float32),
    )(queries, own, self_bias[None])


def finish_kernel(base_ref, a1_ref, a2_ref, b1_ref, b2_ref, gate_ref, gain_ref, out_ref):
    low = a1_ref[...].astype(jnp.float32) + a2_ref[...].astype(jnp.float32)
    high = b1_ref[...].astype(jnp.float32) + b2_ref[...].astype(jnp.float32)
    total = base_ref[...] + jnp.concatenate([low, high], axis=-1)
    average = jnp.mean(total, axis=-1, keepdims=True)
    centered = total - average
    variance = jnp.mean(centered * centered, axis=-1, keepdims=True)
    normed = centered * lax.rsqrt(variance + 1e-05) * gain_ref[...]
    out_ref[...] = (normed * gate_ref[...].astype(jnp.float32)).astype(out_ref.dtype)


def finish(base, low_parts, high_parts, gate, gain):
    rows, width = base.shape
    block = 64
    row_spec = lambda cols: pl.BlockSpec((block, cols), lambda i: (i, 0))
    return pl.pallas_call(
        finish_kernel,
        grid=(rows // block,),
        in_specs=[row_spec(width)]
        + [row_spec(width // 2)] * 4
        + [row_spec(width), pl.BlockSpec((1, width), lambda i: (0, 0))],
        out_specs=row_spec(width),
        out_shape=jax.ShapeDtypeStruct((rows, width), jnp.bfloat16),
    )(base, *low_parts, *high_parts, gate, gain[None])


def per_device(
    cand_query,
    cand_kv,
    cand_gate,
    cache_store,
    holders,
    lengths,
    buckets,
    time_bias,
    self_bias,
    norm_gain,
):
    group_index = lax.axis_index(GROUP)
    y_index = lax.axis_index("yhi")
    y_size = lax.axis_size("yhi")
    z_size = lax.axis_size("z")
    groups = lax.axis_size(GROUP)
    slots, _, piece_len, double_width = cache_store.shape
    holding = (holders // slots).reshape(groups, slots)
    slot_of = (holders % slots).reshape(groups, slots)
    mine = holding == group_index
    chosen = jnp.sum(jnp.where(mine, slot_of, 0), axis=1)
    outgoing = cache_store[chosen, 0]
    incoming = lax.all_to_all(outgoing, GROUP, 0, 0, tiled=True)
    pieces = incoming.reshape(slots * piece_len, double_width)
    history = lax.all_gather(pieces, "z", tiled=True)

    own_holding = lax.dynamic_index_in_dim(holding, group_index, 0, keepdims=False)
    arrived = own_holding[None, :] == jnp.arange(groups, dtype=jnp.int32)[:, None]
    piece_of = jnp.sum(jnp.where(arrived, jnp.arange(slots, dtype=jnp.int32)[None, :], 0), axis=1)
    per_y = z_size * slots * piece_len
    bucket_rows = lax.dynamic_slice_in_dim(buckets[0], y_index * per_y, per_y)
    bucket_rows = bucket_rows.reshape(z_size, slots, piece_len)[:, piece_of].reshape(per_y)
    place = (
        y_index * per_y
        + (jnp.arange(z_size, dtype=jnp.int32) * slots * piece_len)[:, None, None]
        + (piece_of * piece_len)[None, :, None]
        + jnp.arange(piece_len, dtype=jnp.int32)[None, None, :]
    ).reshape(per_y)
    one_hot = (
        bucket_rows[:, None] == jnp.arange(time_bias.shape[0], dtype=jnp.int32)[None, :]
    ).astype(jnp.float32)
    bias = jnp.einsum("kn,nh->hk", one_hot, time_bias, precision=lax.Precision.HIGHEST)
    valid = jnp.broadcast_to(
        (place < lengths[0]).astype(jnp.bfloat16)[:, None], (per_y, HEAD_DIM)
    )

    queries = cand_query[0]
    bias = bias[:, None, :]
    base = own_term(queries, cand_kv[0], self_bias)
    lower, upper, across = (shifted(queries, "yhi", s) for s in (1, -1, 2))
    half = HEADS // 2
    f32, bf16 = jnp.float32, jnp.bfloat16
    (far_low,) = attend([across], history, bias, valid, [bf16], 0, half, 8)
    from_lower = shifted(far_low, "yhi", 1)
    (far_high,) = attend([across], history, bias, valid, [bf16], half, half, 8)
    from_upper = shifted(far_high, "yhi", -1)
    lower_low, upper_low = attend([lower, upper], history, bias, valid, [bf16, f32], 0, half, 8)
    lower_high, upper_high = attend([lower, upper], history, bias, valid, [f32, bf16], half, half, 8)
    low_1 = shifted(lower_low, "yhi", -1)
    high_1 = shifted(upper_high, "yhi", 1)
    low_2 = shifted((upper_low + from_lower.astype(f32)).astype(bf16), "yhi", 1)
    high_2 = shifted((lower_high + from_upper.astype(f32)).astype(bf16), "yhi", -1)
    (total,) = attend([queries], history, bias, valid, [f32], 0, HEADS, 8, base)
    return finish(total, (low_1, low_2), (high_1, high_2), cand_gate[0], norm_gain)[None]


def solution(mesh):
    split = Mesh(mesh.devices.reshape(4, 8, 4, 2, 2), LOOP + GROUP)
    rows = P(GROUP, LOOP, None)
    return jax.shard_map(
        per_device,
        mesh=split,
        in_specs=(
            rows,
            rows,
            rows,
            P(GROUP, LOOP, None, None),
            P(),
            P(GROUP),
            P(GROUP, None),
            P(),
            P(),
            P(),
        ),
        out_specs=rows,
        check_vma=False,
    )
```

```python
import math

import jax
import jax.numpy as jnp
from jax import lax
from jax.experimental import pallas as pl
from jax.experimental.pallas import tpu as pltpu
from jax.sharding import Mesh
from jax.sharding import PartitionSpec as P

HEADS = 16
HEAD_DIM = 128
GROUP = ("x", "ylo", "core")
LOOP = ("yhi", "z")


def shifted(value, axis, steps):
    count = lax.axis_size(axis)
    return lax.ppermute(value, axis, [(i, (i + steps) % count) for i in range(count)])


def make_attend_kernel(blocks, pieces):
    def kernel(*refs):
        q_refs = refs[:blocks]
        k_refs = refs[blocks : blocks + pieces]
        v_refs = refs[blocks + pieces : blocks + 2 * pieces]
        bias_ref, valid_ref, base_ref = refs[blocks + 2 * pieces : blocks + 2 * pieces + 3]
        out_refs = refs[blocks + 2 * pieces + 3 :]
        rows = q_refs[0].shape[0]
        scale = 0.5 / math.sqrt(HEAD_DIM)
        valid = valid_ref[...]
        for head in range(bias_ref.shape[0]):
            cols = slice(head * HEAD_DIM, (head + 1) * HEAD_DIM)
            queries = jnp.concatenate([q_ref[:, cols] for q_ref in q_refs], axis=0)
            keys = jnp.concatenate([k_ref[:, cols] for k_ref in k_refs], axis=0)
            values = jnp.concatenate([v_ref[:, cols] for v_ref in v_refs], axis=0)
            scores = lax.dot_general(
                queries, keys, (((1,), (1,)), ((), ())), preferred_element_type=jnp.float32
            )
            half = scores * scale + bias_ref[head] * 0.5
            weights = (half + half * jnp.tanh(half)).astype(jnp.bfloat16)
            sums = jnp.dot(weights, values * valid, preferred_element_type=jnp.float32)
            for i, out_ref in enumerate(out_refs):
                block = sums[i * rows : (i + 1) * rows]
                if i == 0:
                    block = block + base_ref[:, cols]
                out_ref[:, cols] = block.astype(out_ref.dtype)

    return kernel


def attend(queries, history, bias, valid, base, types, part, parts, per_step):
    rows = queries[0].shape[0]
    positions = valid.shape[0]
    width = per_step * HEAD_DIM
    steps = HEADS // parts // per_step
    skip = part * steps
    out_spec = pl.BlockSpec((rows, width), lambda i: (0, i))
    full_spec = pl.BlockSpec((rows, width), lambda i: (0, i + skip))
    heads = HEADS // parts
    return pl.pallas_call(
        make_attend_kernel(len(queries), len(history)),
        grid=(steps,),
        in_specs=[full_spec] * len(queries)
        + [pl.BlockSpec((h.shape[0], width), lambda i: (0, i)) for h in history]
        + [pl.BlockSpec((h.shape[0], width), lambda i: (0, i + steps)) for h in history]
        + [
            pl.BlockSpec((per_step, 1, positions), lambda i: (i + skip, 0, 0)),
            pl.BlockSpec((positions, HEAD_DIM), lambda i: (0, 0)),
            full_spec,
        ],
        out_specs=[out_spec] * len(queries),
        out_shape=[jax.ShapeDtypeStruct((rows, heads * HEAD_DIM), t) for t in types],
        compiler_params=pltpu.CompilerParams(vmem_limit_bytes=56 * 1024 * 1024),
        cost_estimate=pl.CostEstimate(
            flops=4 * len(queries) * rows * positions * heads * HEAD_DIM,
            bytes_accessed=4 * positions * heads * HEAD_DIM,
            transcendentals=len(queries) * rows * positions * heads,
        ),
    )(*queries, *history, *history, bias, valid, base)


def ring_step(blocks, rows=None):
    up, down = blocks
    if rows is not None:
        up, down = up[:rows], down[rows:]
    return shifted(up, "z", 1), shifted(down, "z", -1)


def own_kernel(q_ref, own_ref, self_bias_ref, out_ref):
    width = q_ref.shape[1]
    scale = 0.5 / math.sqrt(HEAD_DIM)
    for head in range(width // HEAD_DIM):
        cols = slice(head * HEAD_DIM, (head + 1) * HEAD_DIM)
        value_cols = slice(width + head * HEAD_DIM, width + (head + 1) * HEAD_DIM)
        product = q_ref[:, cols].astype(jnp.float32) * own_ref[:, cols].astype(jnp.float32)
        half = jnp.sum(product, axis=-1, keepdims=True) * scale + 0.5 * self_bias_ref[0, head]
        weight = (half + half * jnp.tanh(half)).astype(jnp.bfloat16).astype(jnp.float32)
        out_ref[:, cols] = weight * own_ref[:, value_cols].astype(jnp.float32)


def own_term(queries, own, self_bias):
    rows, width = queries.shape
    block = 32
    return pl.pallas_call(
        own_kernel,
        grid=(rows // block,),
        in_specs=[
            pl.BlockSpec((block, width), lambda i: (i, 0)),
            pl.BlockSpec((block, 2 * width), lambda i: (i, 0)),
            pl.BlockSpec(memory_space=pltpu.SMEM),
        ],
        out_specs=pl.BlockSpec((block, width), lambda i: (i, 0)),
        out_shape=jax.ShapeDtypeStruct((rows, width), jnp.float32),
    )(queries, own, self_bias[None])


def finish_kernel(a0_ref, a1_ref, a2_ref, b0_ref, b1_ref, b2_ref, gate_ref, gain_ref, out_ref):
    low = a0_ref[...] + a1_ref[...].astype(jnp.float32) + a2_ref[...].astype(jnp.float32)
    high = b0_ref[...] + b1_ref[...].astype(jnp.float32) + b2_ref[...].astype(jnp.float32)
    total = jnp.concatenate([low, high], axis=-1)
    average = jnp.mean(total, axis=-1, keepdims=True)
    centered = total - average
    variance = jnp.mean(centered * centered, axis=-1, keepdims=True)
    normed = centered * lax.rsqrt(variance + 1e-05) * gain_ref[...]
    out_ref[...] = (normed * gate_ref[...].astype(jnp.float32)).astype(out_ref.dtype)


def finish(low_parts, high_parts, gate, gain):
    rows, width = gate.shape
    block = 64
    row_spec = lambda cols: pl.BlockSpec((block, cols), lambda i: (i, 0))
    return pl.pallas_call(
        finish_kernel,
        grid=(rows // block,),
        in_specs=[row_spec(width // 2)] * 6
        + [row_spec(width), pl.BlockSpec((1, width), lambda i: (0, 0))],
        out_specs=row_spec(width),
        out_shape=jax.ShapeDtypeStruct((rows, width), jnp.bfloat16),
    )(*low_parts, *high_parts, gate, gain[None])


def per_device(
    cand_query,
    cand_kv,
    cand_gate,
    cache_store,
    holders,
    lengths,
    buckets,
    time_bias,
    self_bias,
    norm_gain,
):
    group_index = lax.axis_index(GROUP)
    y_index = lax.axis_index("yhi")
    y_size = lax.axis_size("yhi")
    z_size = lax.axis_size("z")
    groups = lax.axis_size(GROUP)
    slots, _, piece_len, double_width = cache_store.shape
    holding = (holders // slots).reshape(groups, slots)
    slot_of = (holders % slots).reshape(groups, slots)
    mine = holding == group_index
    chosen = jnp.sum(jnp.where(mine, slot_of, 0), axis=1)
    outgoing = cache_store[chosen, 0]
    incoming = lax.all_to_all(outgoing, GROUP, 0, 0, tiled=True)
    pieces = incoming.reshape(slots * piece_len, double_width)
    quarter = double_width // 4
    first, second = (
        jnp.concatenate(
            [pieces[:, i * quarter : (i + 1) * quarter], pieces[:, (i + 2) * quarter : (i + 3) * quarter]],
            axis=1,
        )
        for i in range(2)
    )
    low_history, high_history = [first], [second]
    low_pair, high_pair = (first, first), (second, second)
    for rows in (None, None, None, slots * piece_len // 2):
        low_pair = ring_step(low_pair, rows)
        high_pair = ring_step(high_pair, rows)
        low_history += low_pair
        high_history += high_pair

    own_holding = lax.dynamic_index_in_dim(holding, group_index, 0, keepdims=False)
    arrived = own_holding[None, :] == jnp.arange(groups, dtype=jnp.int32)[:, None]
    piece_of = jnp.sum(jnp.where(arrived, jnp.arange(slots, dtype=jnp.int32)[None, :], 0), axis=1)
    per_y = z_size * slots * piece_len
    bucket_rows = lax.dynamic_slice_in_dim(buckets[0], y_index * per_y, per_y)
    near = (lax.axis_index("z") - jnp.array([0, 1, -1, 2, -2, 3, -3, 4], jnp.int32)) % z_size
    bucket_rows = bucket_rows.reshape(z_size, slots, piece_len)[near[:, None], piece_of[None, :]]
    bucket_rows = bucket_rows.reshape(per_y)
    place = (
        y_index * per_y
        + (near * slots * piece_len)[:, None, None]
        + (piece_of * piece_len)[None, :, None]
        + jnp.arange(piece_len, dtype=jnp.int32)[None, None, :]
    ).reshape(per_y)
    one_hot = (
        bucket_rows[:, None] == jnp.arange(time_bias.shape[0], dtype=jnp.int32)[None, :]
    ).astype(jnp.float32)
    bias = jnp.einsum("kn,nh->hk", one_hot, time_bias, precision=lax.Precision.HIGHEST)
    valid = jnp.broadcast_to(
        (place < lengths[0]).astype(jnp.bfloat16)[:, None], (per_y, HEAD_DIM)
    )

    queries = cand_query[0]
    bias = bias[:, None, :]
    base = own_term(queries, cand_kv[0], self_bias)
    lower, upper, across = (shifted(queries, "yhi", s) for s in (1, -1, 2))
    f32, bf16 = jnp.float32, jnp.bfloat16
    blocks = [queries, lower, upper, across]
    own_low, lower_low, upper_low, far_low = attend(
        blocks, low_history, bias, valid, base, [f32, bf16, f32, bf16], 0, 2, 4
    )
    from_lower = shifted(far_low, "yhi", 1)
    low_1 = shifted(lower_low, "yhi", -1)
    own_high, lower_high, upper_high, far_high = attend(
        blocks, high_history, bias, valid, base, [f32, f32, bf16, bf16], 1, 2, 4
    )
    from_upper = shifted(far_high, "yhi", -1)
    high_1 = shifted(upper_high, "yhi", 1)
    low_2 = shifted((upper_low + from_lower.astype(f32)).astype(bf16), "yhi", 1)
    high_2 = shifted((lower_high + from_upper.astype(f32)).astype(bf16), "yhi", -1)
    return finish(
        (own_low, low_1, low_2), (own_high, high_1, high_2), cand_gate[0], norm_gain
    )[None]


def solution(mesh):
    split = Mesh(mesh.devices.reshape(4, 8, 4, 2, 2), LOOP + GROUP)
    rows = P(GROUP, LOOP, None)
    return jax.shard_map(
        per_device,
        mesh=split,
        in_specs=(
            rows,
            rows,
            rows,
            P(GROUP, LOOP, None, None),
            P(),
            P(GROUP),
            P(GROUP, None),
            P(),
            P(),
            P(),
        ),
        out_specs=rows,
        check_vma=False,
    )
```

```python
import math

import jax
import jax.numpy as jnp
from jax import lax
from jax.experimental import pallas as pl
from jax.experimental.pallas import tpu as pltpu
from jax.sharding import Mesh
from jax.sharding import PartitionSpec as P

HEADS = 16
HEAD_DIM = 128
GROUP = ("x", "ylo", "core")
LOOP = ("yhi", "z")


def shifted(value, axis, steps):
    count = lax.axis_size(axis)
    return lax.ppermute(value, axis, [(i, (i + steps) % count) for i in range(count)])


def make_attend_kernel(blocks):
    def kernel(*refs):
        q_refs = refs[:blocks]
        k_ref, v_ref, bias_ref, valid_ref, base_ref = refs[blocks : blocks + 5]
        out_refs = refs[blocks + 5 :]
        rows = q_refs[0].shape[0]
        scale = 0.5 / math.sqrt(HEAD_DIM)
        valid = valid_ref[...]
        for head in range(bias_ref.shape[0]):
            cols = slice(head * HEAD_DIM, (head + 1) * HEAD_DIM)
            queries = jnp.concatenate([q_ref[:, cols] for q_ref in q_refs], axis=0)
            scores = lax.dot_general(
                queries,
                k_ref[:, cols],
                (((1,), (1,)), ((), ())),
                preferred_element_type=jnp.float32,
            )
            half = scores * scale + bias_ref[head] * 0.5
            weights = (half + half * jnp.tanh(half)).astype(jnp.bfloat16)
            sums = jnp.dot(weights, v_ref[:, cols] * valid, preferred_element_type=jnp.float32)
            for i, out_ref in enumerate(out_refs):
                block = sums[i * rows : (i + 1) * rows]
                if i == 0:
                    block = block + base_ref[:, cols]
                out_ref[:, cols] = block.astype(out_ref.dtype)

    return kernel


def attend(queries, history, bias, valid, base, types, part, parts, per_step):
    rows = queries[0].shape[0]
    positions = valid.shape[0]
    width = per_step * HEAD_DIM
    heads = HEADS // parts
    steps = heads // per_step
    skip = part * steps
    all_steps = HEADS // per_step
    out_spec = pl.BlockSpec((rows, width), lambda i: (0, i))
    full_spec = pl.BlockSpec((rows, width), lambda i: (0, i + skip))
    return pl.pallas_call(
        make_attend_kernel(len(queries)),
        grid=(steps,),
        in_specs=[full_spec] * len(queries)
        + [
            pl.BlockSpec((positions, width), lambda i: (0, i + skip)),
            pl.BlockSpec((positions, width), lambda i: (0, i + skip + all_steps)),
            pl.BlockSpec((per_step, 1, positions), lambda i: (i + skip, 0, 0)),
            pl.BlockSpec((positions, HEAD_DIM), lambda i: (0, 0)),
            full_spec,
        ],
        out_specs=[out_spec] * len(queries),
        out_shape=[jax.ShapeDtypeStruct((rows, heads * HEAD_DIM), t) for t in types],
        compiler_params=pltpu.CompilerParams(vmem_limit_bytes=56 * 1024 * 1024),
        cost_estimate=pl.CostEstimate(
            flops=4 * len(queries) * rows * positions * heads * HEAD_DIM,
            bytes_accessed=4 * positions * heads * HEAD_DIM,
            transcendentals=len(queries) * rows * positions * heads,
        ),
    )(*queries, history, history, bias, valid, base)


def own_kernel(q_ref, own_ref, self_bias_ref, out_ref):
    width = q_ref.shape[1]
    scale = 0.5 / math.sqrt(HEAD_DIM)
    for head in range(width // HEAD_DIM):
        cols = slice(head * HEAD_DIM, (head + 1) * HEAD_DIM)
        value_cols = slice(width + head * HEAD_DIM, width + (head + 1) * HEAD_DIM)
        product = q_ref[:, cols].astype(jnp.float32) * own_ref[:, cols].astype(jnp.float32)
        half = jnp.sum(product, axis=-1, keepdims=True) * scale + 0.5 * self_bias_ref[0, head]
        weight = (half + half * jnp.tanh(half)).astype(jnp.bfloat16).astype(jnp.float32)
        out_ref[:, cols] = weight * own_ref[:, value_cols].astype(jnp.float32)


def own_term(queries, own, self_bias):
    rows, width = queries.shape
    block = 32
    return pl.pallas_call(
        own_kernel,
        grid=(rows // block,),
        in_specs=[
            pl.BlockSpec((block, width), lambda i: (i, 0)),
            pl.BlockSpec((block, 2 * width), lambda i: (i, 0)),
            pl.BlockSpec(memory_space=pltpu.SMEM),
        ],
        out_specs=pl.BlockSpec((block, width), lambda i: (i, 0)),
        out_shape=jax.ShapeDtypeStruct((rows, width), jnp.float32),
    )(queries, own, self_bias[None])


def finish_kernel(a0_ref, a1_ref, a2_ref, b0_ref, b1_ref, b2_ref, gate_ref, gain_ref, out_ref):
    low = a0_ref[...] + a1_ref[...].astype(jnp.float32) + a2_ref[...].astype(jnp.float32)
    high = b0_ref[...] + b1_ref[...].astype(jnp.float32) + b2_ref[...].astype(jnp.float32)
    total = jnp.concatenate([low, high], axis=-1)
    average = jnp.mean(total, axis=-1, keepdims=True)
    centered = total - average
    variance = jnp.mean(centered * centered, axis=-1, keepdims=True)
    normed = centered * lax.rsqrt(variance + 1e-05) * gain_ref[...]
    out_ref[...] = (normed * gate_ref[...].astype(jnp.float32)).astype(out_ref.dtype)


def finish(low_parts, high_parts, gate, gain):
    rows, width = gate.shape
    block = 64
    row_spec = lambda cols: pl.BlockSpec((block, cols), lambda i: (i, 0))
    return pl.pallas_call(
        finish_kernel,
        grid=(rows // block,),
        in_specs=[row_spec(width // 2)] * 6
        + [row_spec(width), pl.BlockSpec((1, width), lambda i: (0, 0))],
        out_specs=row_spec(width),
        out_shape=jax.ShapeDtypeStruct((rows, width), jnp.bfloat16),
    )(*low_parts, *high_parts, gate, gain[None])


def per_device(
    cand_query,
    cand_kv,
    cand_gate,
    cache_store,
    holders,
    lengths,
    buckets,
    time_bias,
    self_bias,
    norm_gain,
):
    group_index = lax.axis_index(GROUP)
    y_index = lax.axis_index("yhi")
    y_size = lax.axis_size("yhi")
    z_size = lax.axis_size("z")
    groups = lax.axis_size(GROUP)
    slots, _, piece_len, double_width = cache_store.shape
    holding = (holders // slots).reshape(groups, slots)
    slot_of = (holders % slots).reshape(groups, slots)
    mine = holding == group_index
    chosen = jnp.sum(jnp.where(mine, slot_of, 0), axis=1)
    outgoing = cache_store[chosen, 0]
    incoming = lax.all_to_all(outgoing, GROUP, 0, 0, tiled=True)
    pieces = incoming.reshape(slots * piece_len, double_width)
    history = lax.all_gather(pieces, "z", tiled=True)

    own_holding = lax.dynamic_index_in_dim(holding, group_index, 0, keepdims=False)
    arrived = own_holding[None, :] == jnp.arange(groups, dtype=jnp.int32)[:, None]
    piece_of = jnp.sum(jnp.where(arrived, jnp.arange(slots, dtype=jnp.int32)[None, :], 0), axis=1)
    per_y = z_size * slots * piece_len
    bucket_rows = lax.dynamic_slice_in_dim(buckets[0], y_index * per_y, per_y)
    bucket_rows = bucket_rows.reshape(z_size, slots, piece_len)[:, piece_of].reshape(per_y)
    place = (
        y_index * per_y
        + (jnp.arange(z_size, dtype=jnp.int32) * slots * piece_len)[:, None, None]
        + (piece_of * piece_len)[None, :, None]
        + jnp.arange(piece_len, dtype=jnp.int32)[None, None, :]
    ).reshape(per_y)
    one_hot = (
        bucket_rows[:, None] == jnp.arange(time_bias.shape[0], dtype=jnp.int32)[None, :]
    ).astype(jnp.float32)
    bias = jnp.einsum("kn,nh->hk", one_hot, time_bias, precision=lax.Precision.HIGHEST)
    valid = jnp.broadcast_to(
        (place < lengths[0]).astype(jnp.bfloat16)[:, None], (per_y, HEAD_DIM)
    )

    queries = cand_query[0]
    bias = bias[:, None, :]
    base = own_term(queries, cand_kv[0], self_bias)
    lower, upper, across = (shifted(queries, "yhi", s) for s in (1, -1, 2))
    f32, bf16 = jnp.float32, jnp.bfloat16
    blocks = [queries, lower, upper, across]
    own_low, lower_low, upper_low, far_low = attend(
        blocks, history, bias, valid, base, [f32, bf16, f32, bf16], 0, 2, 4
    )
    from_lower = shifted(far_low, "yhi", 1)
    low_1 = shifted(lower_low, "yhi", -1)
    own_high, lower_high, upper_high, far_high = attend(
        blocks, history, bias, valid, base, [f32, f32, bf16, bf16], 1, 2, 4
    )
    from_upper = shifted(far_high, "yhi", -1)
    high_1 = shifted(upper_high, "yhi", 1)
    low_2 = shifted((upper_low + from_lower.astype(f32)).astype(bf16), "yhi", 1)
    high_2 = shifted((lower_high + from_upper.astype(f32)).astype(bf16), "yhi", -1)
    return finish(
        (own_low, low_1, low_2), (own_high, high_1, high_2), cand_gate[0], norm_gain
    )[None]


def solution(mesh):
    split = Mesh(mesh.devices.reshape(4, 8, 4, 2, 2), LOOP + GROUP)
    rows = P(GROUP, LOOP, None)
    return jax.shard_map(
        per_device,
        mesh=split,
        in_specs=(
            rows,
            rows,
            rows,
            P(GROUP, LOOP, None, None),
            P(),
            P(GROUP),
            P(GROUP, None),
            P(),
            P(),
            P(),
        ),
        out_specs=rows,
        check_vma=False,
    )
```

```python
import math

import jax
import jax.numpy as jnp
from jax import lax
from jax.experimental import pallas as pl
from jax.experimental.pallas import tpu as pltpu
from jax.sharding import Mesh
from jax.sharding import PartitionSpec as P

HEADS = 16
HEAD_DIM = 128
GROUP = ("x", "ylo", "core")
LOOP = ("yh1", "yh0", "z")
Y = ("yh1", "yh0")


def attend_kernel(q_ref, k_ref, v_ref, bias_ref, mask_ref, out_ref):
    blocks, rows, width = q_ref.shape
    scale = 0.5 / math.sqrt(HEAD_DIM)
    inside = mask_ref[...] > 0.0
    for head in range(width // HEAD_DIM):
        cols = slice(head * HEAD_DIM, (head + 1) * HEAD_DIM)
        queries = q_ref[:, :, cols].reshape(blocks * rows, HEAD_DIM)
        scores = lax.dot_general(
            queries, k_ref[:, cols], (((1,), (1,)), ((), ())), preferred_element_type=jnp.float32
        )
        half = scores * scale + bias_ref[head]
        weights = jnp.where(inside, half + half * jnp.tanh(half), 0.0).astype(jnp.bfloat16)
        sums = jnp.dot(weights, v_ref[:, cols], preferred_element_type=jnp.float32)
        out_ref[:, :, cols] = sums.reshape(blocks, rows, HEAD_DIM).astype(out_ref.dtype)


def attend(queries, history, bias, mask, per_step):
    blocks, rows, full = queries.shape
    positions = history.shape[0]
    width = per_step * HEAD_DIM
    steps = full // width
    return pl.pallas_call(
        attend_kernel,
        grid=(steps,),
        in_specs=[
            pl.BlockSpec((blocks, rows, width), lambda i: (0, 0, i)),
            pl.BlockSpec((positions, width), lambda i: (0, i)),
            pl.BlockSpec((positions, width), lambda i: (0, i + steps)),
            pl.BlockSpec((per_step, 1, positions), lambda i: (i, 0, 0)),
            pl.BlockSpec((1, positions), lambda i: (0, 0)),
        ],
        out_specs=pl.BlockSpec((blocks, rows, width), lambda i: (0, 0, i)),
        out_shape=jax.ShapeDtypeStruct((blocks, rows, full), jnp.bfloat16),
        compiler_params=pltpu.CompilerParams(vmem_limit_bytes=56 * 1024 * 1024),
        cost_estimate=pl.CostEstimate(
            flops=4 * blocks * rows * positions * full,
            bytes_accessed=4 * positions * full + 4 * blocks * rows * full,
            transcendentals=blocks * rows * positions * full // HEAD_DIM,
        ),
    )(queries, history, history, bias, mask)


def own_kernel(q_ref, own_ref, self_bias_ref, out_ref):
    width = q_ref.shape[1]
    scale = 0.5 / math.sqrt(HEAD_DIM)
    for head in range(width // HEAD_DIM):
        cols = slice(head * HEAD_DIM, (head + 1) * HEAD_DIM)
        value_cols = slice(width + head * HEAD_DIM, width + (head + 1) * HEAD_DIM)
        product = q_ref[:, cols].astype(jnp.float32) * own_ref[:, cols].astype(jnp.float32)
        half = jnp.sum(product, axis=-1, keepdims=True) * scale + 0.5 * self_bias_ref[0, head]
        weight = (half + half * jnp.tanh(half)).astype(jnp.bfloat16).astype(jnp.float32)
        out_ref[:, cols] = weight * own_ref[:, value_cols].astype(jnp.float32)


def own_term(queries, own, self_bias):
    rows, width = queries.shape
    block = 32
    return pl.pallas_call(
        own_kernel,
        grid=(rows // block,),
        in_specs=[
            pl.BlockSpec((block, width), lambda i: (i, 0)),
            pl.BlockSpec((block, 2 * width), lambda i: (i, 0)),
            pl.BlockSpec(memory_space=pltpu.SMEM),
        ],
        out_specs=pl.BlockSpec((block, width), lambda i: (i, 0)),
        out_shape=jax.ShapeDtypeStruct((rows, width), jnp.float32),
    )(queries, own, self_bias[None])


def finish_kernel(core_ref, parts_ref, other_ref, base_ref, gate_ref, gain_ref, out_ref):
    first_core = core_ref[0] == 0
    a, b, c, d = (parts_ref[i].astype(jnp.float32) for i in range(4))
    mine = jnp.where(first_core, a + b, c + d)
    other = other_ref[...].astype(jnp.float32)
    low = jnp.where(first_core, mine, other)
    high = jnp.where(first_core, other, mine)
    total = base_ref[...] + jnp.concatenate([low, high], axis=-1)
    average = jnp.mean(total, axis=-1, keepdims=True)
    centered = total - average
    variance = jnp.mean(centered * centered, axis=-1, keepdims=True)
    normed = centered * lax.rsqrt(variance + 1e-05) * gain_ref[...]
    out_ref[...] = (normed * gate_ref[...].astype(jnp.float32)).astype(out_ref.dtype)


def finish(core, parts, other, base, gate, gain):
    rows, width = gate.shape
    block = 64
    row_spec = lambda cols: pl.BlockSpec((block, cols), lambda i: (i, 0))
    return pl.pallas_call(
        finish_kernel,
        grid=(rows // block,),
        in_specs=[
            pl.BlockSpec(memory_space=pltpu.SMEM),
            pl.BlockSpec((4, block, width // 2), lambda i: (0, i, 0)),
            row_spec(width // 2),
            row_spec(width),
            row_spec(width),
            pl.BlockSpec((1, width), lambda i: (0, 0)),
        ],
        out_specs=row_spec(width),
        out_shape=jax.ShapeDtypeStruct((rows, width), jnp.bfloat16),
    )(core[None], parts, other, base, gate, gain[None])


def swapped(value):
    return lax.ppermute(value, "core", [(0, 1), (1, 0)])


def per_device(
    cand_query,
    cand_kv,
    cand_gate,
    cache_store,
    holders,
    lengths,
    buckets,
    time_bias,
    self_bias,
    norm_gain,
):
    core = lax.axis_index("core")
    side = lax.axis_index("yh1")
    half_y = lax.axis_index("yh0")
    group_index = lax.axis_index(GROUP)
    groups = lax.axis_size(GROUP)
    z_size = lax.axis_size("z")
    slots, _, piece_len, double_width = cache_store.shape
    width = double_width // 2
    half_width = width // 2

    holding = (holders // slots).reshape(groups, slots)
    slot_of = (holders % slots).reshape(groups, slots)
    chosen = jnp.sum(jnp.where(holding == group_index, slot_of, 0), axis=1)
    by_half = jnp.stack(
        [
            jnp.concatenate(
                [
                    cache_store[:, 0, :, h * half_width : (h + 1) * half_width],
                    cache_store[:, 0, :, width + h * half_width : width + (h + 1) * half_width],
                ],
                axis=-1,
            )
            for h in range(2)
        ]
    ).reshape(2 * slots, piece_len, width)
    places = chosen.reshape(groups // 2, 2).T[:, :, None] + slots * jnp.arange(2, dtype=jnp.int32)
    outgoing = by_half[places.reshape(-1)]
    incoming = lax.all_to_all(outgoing, ("yh1",) + GROUP, 0, 0, tiled=True)
    pieces = incoming.reshape(2 * groups * piece_len, width)
    history = lax.all_gather(pieces, "z", tiled=True)

    queries = cand_query[0]
    own_half = lax.dynamic_slice_in_dim(queries, core * half_width, half_width, 1)
    other_half = lax.dynamic_slice_in_dim(queries, (1 - core) * half_width, half_width, 1)
    partner_half = swapped(other_half)
    first = jnp.where(core == 0, own_half, partner_half)
    second = jnp.where(core == 0, partner_half, own_half)
    spread = lax.all_to_all(jnp.stack([first, first, second, second]), Y, 0, 0, tiled=True)

    about = jnp.concatenate([buckets[0], lengths])
    about = jnp.where(core == side, about, swapped(about))
    session = (group_index // 2) * 2 + side
    own_holding = lax.dynamic_index_in_dim(holding, session, 0, keepdims=False)
    arrived = own_holding[None, :] == jnp.arange(groups, dtype=jnp.int32)[:, None]
    piece_of = jnp.sum(jnp.where(arrived, jnp.arange(slots, dtype=jnp.int32)[None, :], 0), axis=1)
    order = jnp.arange(z_size, dtype=jnp.int32)[:, None, None, None]
    order = order + (2 * jnp.arange(2, dtype=jnp.int32)[None, :, None, None] + half_y) * z_size
    place = (
        (order * slots + piece_of[None, None, :, None]) * piece_len
        + jnp.arange(piece_len, dtype=jnp.int32)[None, None, None, :]
    ).reshape(-1)
    mask = (place < about[-1]).astype(jnp.float32)[None, :]
    one_hot = (
        about[place][:, None] == jnp.arange(time_bias.shape[0], dtype=jnp.int32)[None, :]
    ).astype(jnp.float32)
    own_bias = lax.dynamic_slice_in_dim(time_bias, core * (HEADS // 2), HEADS // 2, 1)
    bias = 0.5 * jnp.einsum("kn,nh->hk", one_hot, own_bias, precision=lax.Precision.HIGHEST)

    base = own_term(queries, cand_kv[0], self_bias)
    partial = attend(spread, history, bias[:, None, :], mask, 2)
    parts = lax.all_to_all(partial, Y, 0, 0, tiled=True)
    pair = lax.dynamic_slice_in_dim(parts, 2 * (1 - core), 2).astype(jnp.float32)
    other = swapped((pair[0] + pair[1]).astype(jnp.bfloat16))
    return finish(core, parts, other, base, cand_gate[0], norm_gain)[None]


def solution(mesh):
    split = Mesh(mesh.devices.reshape(2, 2, 8, 4, 2, 2), LOOP + GROUP)
    rows = P(GROUP, LOOP, None)
    return jax.shard_map(
        per_device,
        mesh=split,
        in_specs=(
            rows,
            rows,
            rows,
            P(GROUP, LOOP, None, None),
            P(),
            P(GROUP),
            P(GROUP, None),
            P(),
            P(),
            P(),
        ),
        out_specs=rows,
        check_vma=False,
    )
```

```python
import math

import jax
import jax.numpy as jnp
from jax import lax
from jax.experimental import pallas as pl
from jax.experimental.pallas import tpu as pltpu
from jax.sharding import Mesh
from jax.sharding import PartitionSpec as P

HEADS = 16
HEAD_DIM = 128
GROUP = ("x", "ylo", "core")
LOOP = ("yh1", "yh0", "z")
Y = ("yh1", "yh0")


def attend_kernel(q_ref, k_ref, v_ref, bias_ref, mask_ref, out_ref):
    blocks, rows, width = q_ref.shape
    scale = 0.5 / math.sqrt(HEAD_DIM)
    inside = mask_ref[...] > 0.0
    for head in range(width // HEAD_DIM):
        cols = slice(head * HEAD_DIM, (head + 1) * HEAD_DIM)
        queries = q_ref[:, :, cols].reshape(blocks * rows, HEAD_DIM)
        scores = lax.dot_general(
            queries, k_ref[:, cols], (((1,), (1,)), ((), ())), preferred_element_type=jnp.float32
        )
        half = scores * scale + bias_ref[head]
        weights = jnp.where(inside, half + half * jnp.tanh(half), 0.0).astype(jnp.bfloat16)
        sums = jnp.dot(weights, v_ref[:, cols], preferred_element_type=jnp.float32)
        out_ref[:, :, cols] = sums.reshape(blocks, rows, HEAD_DIM).astype(out_ref.dtype)


def attend(queries, history, bias, mask, part, parts, per_step):
    blocks, rows, full = queries.shape
    positions = history.shape[0]
    width = per_step * HEAD_DIM
    all_steps = full // width
    full = full // parts
    steps = full // width
    skip = part * steps
    return pl.pallas_call(
        attend_kernel,
        grid=(steps,),
        in_specs=[
            pl.BlockSpec((blocks, rows, width), lambda i: (0, 0, i + skip)),
            pl.BlockSpec((positions, width), lambda i: (0, i + skip)),
            pl.BlockSpec((positions, width), lambda i: (0, i + skip + all_steps)),
            pl.BlockSpec((per_step, 1, positions), lambda i: (i + skip, 0, 0)),
            pl.BlockSpec((1, positions), lambda i: (0, 0)),
        ],
        out_specs=pl.BlockSpec((blocks, rows, width), lambda i: (0, 0, i)),
        out_shape=jax.ShapeDtypeStruct((blocks, rows, full), jnp.bfloat16),
        compiler_params=pltpu.CompilerParams(vmem_limit_bytes=56 * 1024 * 1024),
        cost_estimate=pl.CostEstimate(
            flops=4 * blocks * rows * positions * full,
            bytes_accessed=4 * positions * full + 4 * blocks * rows * full,
            transcendentals=blocks * rows * positions * full // HEAD_DIM,
        ),
    )(queries, history, history, bias, mask)


def own_kernel(q_ref, own_ref, self_bias_ref, out_ref):
    width = q_ref.shape[1]
    scale = 0.5 / math.sqrt(HEAD_DIM)
    for head in range(width // HEAD_DIM):
        cols = slice(head * HEAD_DIM, (head + 1) * HEAD_DIM)
        value_cols = slice(width + head * HEAD_DIM, width + (head + 1) * HEAD_DIM)
        product = q_ref[:, cols].astype(jnp.float32) * own_ref[:, cols].astype(jnp.float32)
        half = jnp.sum(product, axis=-1, keepdims=True) * scale + 0.5 * self_bias_ref[0, head]
        weight = (half + half * jnp.tanh(half)).astype(jnp.bfloat16).astype(jnp.float32)
        out_ref[:, cols] = weight * own_ref[:, value_cols].astype(jnp.float32)


def own_term(queries, own, self_bias):
    rows, width = queries.shape
    block = 32
    return pl.pallas_call(
        own_kernel,
        grid=(rows // block,),
        in_specs=[
            pl.BlockSpec((block, width), lambda i: (i, 0)),
            pl.BlockSpec((block, 2 * width), lambda i: (i, 0)),
            pl.BlockSpec(memory_space=pltpu.SMEM),
        ],
        out_specs=pl.BlockSpec((block, width), lambda i: (i, 0)),
        out_shape=jax.ShapeDtypeStruct((rows, width), jnp.float32),
    )(queries, own, self_bias[None])


def finish_kernel(core_ref, low_ref, high_ref, other_low_ref, other_high_ref, base_ref, gate_ref, gain_ref, out_ref):
    first_core = core_ref[0] == 0
    halves = []
    for parts_ref in (low_ref, high_ref):
        a, b, c, d = (parts_ref[i].astype(jnp.float32) for i in range(4))
        halves.append(jnp.where(first_core, a + d, b + c))
    mine = jnp.concatenate(halves, axis=-1)
    other = jnp.concatenate([other_low_ref[...], other_high_ref[...]], axis=-1).astype(jnp.float32)
    low = jnp.where(first_core, mine, other)
    high = jnp.where(first_core, other, mine)
    total = base_ref[...] + jnp.concatenate([low, high], axis=-1)
    average = jnp.mean(total, axis=-1, keepdims=True)
    centered = total - average
    variance = jnp.mean(centered * centered, axis=-1, keepdims=True)
    normed = centered * lax.rsqrt(variance + 1e-05) * gain_ref[...]
    out_ref[...] = (normed * gate_ref[...].astype(jnp.float32)).astype(out_ref.dtype)


def finish(core, parts, others, base, gate, gain):
    rows, width = gate.shape
    block = 64
    row_spec = lambda cols: pl.BlockSpec((block, cols), lambda i: (i, 0))
    return pl.pallas_call(
        finish_kernel,
        grid=(rows // block,),
        in_specs=[pl.BlockSpec(memory_space=pltpu.SMEM)]
        + [pl.BlockSpec((4, block, width // 4), lambda i: (0, i, 0))] * 2
        + [row_spec(width // 4)] * 2
        + [row_spec(width), row_spec(width), pl.BlockSpec((1, width), lambda i: (0, 0))],
        out_specs=row_spec(width),
        out_shape=jax.ShapeDtypeStruct((rows, width), jnp.bfloat16),
    )(core[None], *parts, *others, base, gate, gain[None])


def swapped(value):
    return lax.ppermute(value, "core", [(0, 1), (1, 0)])


def per_device(
    cand_query,
    cand_kv,
    cand_gate,
    cache_store,
    holders,
    lengths,
    buckets,
    time_bias,
    self_bias,
    norm_gain,
):
    core = lax.axis_index("core")
    upper_y = lax.axis_index("yh1")
    side = upper_y ^ lax.axis_index("yh0")
    group_index = lax.axis_index(GROUP)
    groups = lax.axis_size(GROUP)
    z_size = lax.axis_size("z")
    slots, _, piece_len, double_width = cache_store.shape
    width = double_width // 2
    half_width = width // 2

    holding = (holders // slots).reshape(groups, slots)
    slot_of = (holders % slots).reshape(groups, slots)
    chosen = jnp.sum(jnp.where(holding == group_index, slot_of, 0), axis=1).reshape(groups // 2, 2).T
    chosen = jnp.where(upper_y == 0, chosen, chosen[::-1]).reshape(-1)
    picked = cache_store[chosen, 0].reshape(groups, 1, piece_len, double_width)
    outgoing = jnp.concatenate(
        [
            jnp.concatenate(
                [
                    picked[..., h * half_width : (h + 1) * half_width],
                    picked[..., width + h * half_width : width + (h + 1) * half_width],
                ],
                axis=-1,
            )
            for h in range(2)
        ],
        axis=1,
    ).reshape(2 * groups, piece_len, width)
    incoming = lax.all_to_all(outgoing, ("yh0",) + GROUP, 0, 0, tiled=True)
    pieces = incoming.reshape(2 * groups * piece_len, width)
    history = lax.all_gather(pieces, "z", tiled=True)

    queries = cand_query[0]
    own_half = lax.dynamic_slice_in_dim(queries, core * half_width, half_width, 1)
    other_half = lax.dynamic_slice_in_dim(queries, (1 - core) * half_width, half_width, 1)
    partner_half = swapped(other_half)
    first = jnp.where(core == 0, own_half, partner_half)
    second = jnp.where(core == 0, partner_half, own_half)
    spread = lax.all_to_all(jnp.stack([first, second, second, first]), Y, 0, 0, tiled=True)

    about = jnp.concatenate([buckets[0], lengths])
    about = jnp.where(core == side, about, swapped(about))
    session = (group_index // 2) * 2 + side
    own_holding = lax.dynamic_index_in_dim(holding, session, 0, keepdims=False)
    arrived = own_holding[None, :] == jnp.arange(groups, dtype=jnp.int32)[:, None]
    piece_of = jnp.sum(jnp.where(arrived, jnp.arange(slots, dtype=jnp.int32)[None, :], 0), axis=1)
    order = jnp.arange(z_size, dtype=jnp.int32)[:, None, None, None]
    order = order + (jnp.arange(2, dtype=jnp.int32)[None, :, None, None] + 2 * upper_y) * z_size
    place = (
        (order * slots + piece_of[None, None, :, None]) * piece_len
        + jnp.arange(piece_len, dtype=jnp.int32)[None, None, None, :]
    ).reshape(-1)
    mask = (place < about[-1]).astype(jnp.float32)[None, :]
    one_hot = (
        about[place][:, None] == jnp.arange(time_bias.shape[0], dtype=jnp.int32)[None, :]
    ).astype(jnp.float32)
    own_bias = lax.dynamic_slice_in_dim(time_bias, core * (HEADS // 2), HEADS // 2, 1)
    bias = 0.5 * jnp.einsum("kn,nh->hk", one_hot, own_bias, precision=lax.Precision.HIGHEST)

    base = own_term(queries, cand_kv[0], self_bias)
    bias, mask, base = lax.optimization_barrier((bias[:, None, :], mask, base))
    parts, others = [], []
    for part in range(2):
        partial = attend(spread, history, bias, mask, part, 2, 2)
        came = lax.all_to_all(partial, Y, 0, 0, tiled=True)
        a, b, c, d = (came[i].astype(jnp.float32) for i in range(4))
        parts.append(came)
        others.append(swapped(jnp.where(core == 0, b + c, a + d).astype(jnp.bfloat16)))
    return finish(core, parts, others, base, cand_gate[0], norm_gain)[None]


def solution(mesh):
    split = Mesh(mesh.devices.reshape(2, 2, 8, 4, 2, 2), LOOP + GROUP)
    rows = P(GROUP, LOOP, None)
    return jax.shard_map(
        per_device,
        mesh=split,
        in_specs=(
            rows,
            rows,
            rows,
            P(GROUP, LOOP, None, None),
            P(),
            P(GROUP),
            P(GROUP, None),
            P(),
            P(),
            P(),
        ),
        out_specs=rows,
        check_vma=False,
    )
```

```python
import math

import jax
import jax.numpy as jnp
from jax import lax
from jax.experimental import pallas as pl
from jax.experimental.pallas import tpu as pltpu
from jax.sharding import Mesh
from jax.sharding import PartitionSpec as P

HEADS = 16
HEAD_DIM = 128
GROUP = ("x", "ylo", "core")
LOOP = ("yh1", "yh0", "z")
Y = ("yh1", "yh0")


HOMES = {(0, 0): (1, 3, 2, 0), (0, 1): (0, 1, 3, 2), (3, 0): (2, 0, 1, 3), (3, 1): (3, 2, 0, 1)}


def send_pairs(step):
    pairs = []
    for (yhi, core), homes in HOMES.items():
        pairs.append((yhi * 2 + core, homes[step] * 2))
        pairs.append(((yhi + 2) % 4 * 2 + 1 - core, (homes[step] + 2) % 4 * 2 + 1))
    return pairs


def send_order():
    order = [None] * 8
    for (yhi, core), homes in HOMES.items():
        order[yhi * 2 + core] = list(homes)
        order[(yhi + 2) % 4 * 2 + 1 - core] = [(home + 2) % 4 for home in homes]
    return jnp.array(order, jnp.int32)


def attend_kernel(order_ref, q_ref, k_ref, v_ref, bias_ref, mask_ref, *out_refs):
    blocks, rows, width = q_ref.shape
    scale = 0.5 / math.sqrt(HEAD_DIM)
    inside = mask_ref[...] > 0.0
    for head in range(width // HEAD_DIM):
        cols = slice(head * HEAD_DIM, (head + 1) * HEAD_DIM)
        queries = jnp.concatenate([q_ref[order_ref[i], :, cols] for i in range(blocks)], axis=0)
        scores = lax.dot_general(
            queries, k_ref[:, cols], (((1,), (1,)), ((), ())), preferred_element_type=jnp.float32
        )
        half = scores * scale + bias_ref[head]
        weights = jnp.where(inside, half + half * jnp.tanh(half), 0.0).astype(jnp.bfloat16)
        sums = jnp.dot(weights, v_ref[:, cols], preferred_element_type=jnp.float32)
        for i, out_ref in enumerate(out_refs):
            out_ref[:, cols] = sums[i * rows : (i + 1) * rows].astype(out_ref.dtype)


def attend(order, queries, history, bias, mask, per_step):
    blocks, rows, full = queries.shape
    positions = history.shape[0]
    width = per_step * HEAD_DIM
    steps = full // width
    return pl.pallas_call(
        attend_kernel,
        grid=(steps,),
        in_specs=[
            pl.BlockSpec(memory_space=pltpu.SMEM),
            pl.BlockSpec((blocks, rows, width), lambda i: (0, 0, i)),
            pl.BlockSpec((positions, width), lambda i: (0, i)),
            pl.BlockSpec((positions, width), lambda i: (0, i + steps)),
            pl.BlockSpec((per_step, 1, positions), lambda i: (i, 0, 0)),
            pl.BlockSpec((1, positions), lambda i: (0, 0)),
        ],
        out_specs=[pl.BlockSpec((rows, width), lambda i: (0, i))] * blocks,
        out_shape=[jax.ShapeDtypeStruct((rows, full), jnp.bfloat16)] * blocks,
        compiler_params=pltpu.CompilerParams(vmem_limit_bytes=56 * 1024 * 1024),
        cost_estimate=pl.CostEstimate(
            flops=4 * blocks * rows * positions * full,
            bytes_accessed=4 * positions * full + 4 * blocks * rows * full,
            transcendentals=blocks * rows * positions * full // HEAD_DIM,
        ),
    )(order, queries, history, history, bias, mask)


def own_kernel(q_ref, own_ref, self_bias_ref, out_ref):
    width = q_ref.shape[1]
    scale = 0.5 / math.sqrt(HEAD_DIM)
    for head in range(width // HEAD_DIM):
        cols = slice(head * HEAD_DIM, (head + 1) * HEAD_DIM)
        value_cols = slice(width + head * HEAD_DIM, width + (head + 1) * HEAD_DIM)
        product = q_ref[:, cols].astype(jnp.float32) * own_ref[:, cols].astype(jnp.float32)
        half = jnp.sum(product, axis=-1, keepdims=True) * scale + 0.5 * self_bias_ref[0, head]
        weight = (half + half * jnp.tanh(half)).astype(jnp.bfloat16).astype(jnp.float32)
        out_ref[:, cols] = weight * own_ref[:, value_cols].astype(jnp.float32)


def own_term(queries, own, self_bias):
    rows, width = queries.shape
    block = 32
    return pl.pallas_call(
        own_kernel,
        grid=(rows // block,),
        in_specs=[
            pl.BlockSpec((block, width), lambda i: (i, 0)),
            pl.BlockSpec((block, 2 * width), lambda i: (i, 0)),
            pl.BlockSpec(memory_space=pltpu.SMEM),
        ],
        out_specs=pl.BlockSpec((block, width), lambda i: (i, 0)),
        out_shape=jax.ShapeDtypeStruct((rows, width), jnp.float32),
    )(queries, own, self_bias[None])


def finish_kernel(flag_ref, a_ref, b_ref, c_ref, d_ref, base_ref, gate_ref, gain_ref, out_ref):
    a, b, c, d = (ref[...].astype(jnp.float32) for ref in (a_ref, b_ref, c_ref, d_ref))
    odd, even = a + c, b + d
    even_low = flag_ref[0] == 1
    low = jnp.where(even_low, even, odd)
    high = jnp.where(even_low, odd, even)
    total = base_ref[...] + jnp.concatenate([low, high], axis=-1)
    average = jnp.mean(total, axis=-1, keepdims=True)
    centered = total - average
    variance = jnp.mean(centered * centered, axis=-1, keepdims=True)
    normed = centered * lax.rsqrt(variance + 1e-05) * gain_ref[...]
    out_ref[...] = (normed * gate_ref[...].astype(jnp.float32)).astype(out_ref.dtype)


def finish(flag, parts, base, gate, gain):
    rows, width = gate.shape
    block = 64
    row_spec = lambda cols: pl.BlockSpec((block, cols), lambda i: (i, 0))
    return pl.pallas_call(
        finish_kernel,
        grid=(rows // block,),
        in_specs=[pl.BlockSpec(memory_space=pltpu.SMEM)]
        + [row_spec(width // 2)] * 4
        + [row_spec(width), row_spec(width), pl.BlockSpec((1, width), lambda i: (0, 0))],
        out_specs=row_spec(width),
        out_shape=jax.ShapeDtypeStruct((rows, width), jnp.bfloat16),
    )(flag[None], *parts, base, gate, gain[None])


def swapped(value):
    return lax.ppermute(value, "core", [(0, 1), (1, 0)])


def per_device(
    cand_query,
    cand_kv,
    cand_gate,
    cache_store,
    holders,
    lengths,
    buckets,
    time_bias,
    self_bias,
    norm_gain,
):
    core = lax.axis_index("core")
    upper_y = lax.axis_index("yh1")
    side = upper_y ^ lax.axis_index("yh0")
    group_index = lax.axis_index(GROUP)
    groups = lax.axis_size(GROUP)
    z_size = lax.axis_size("z")
    slots, _, piece_len, double_width = cache_store.shape
    width = double_width // 2
    half_width = width // 2

    holding = (holders // slots).reshape(groups, slots)
    slot_of = (holders % slots).reshape(groups, slots)
    chosen = jnp.sum(jnp.where(holding == group_index, slot_of, 0), axis=1).reshape(groups // 2, 2).T
    chosen = jnp.where(upper_y == 0, chosen, chosen[::-1]).reshape(-1)
    picked = cache_store[chosen, 0].reshape(groups, 1, piece_len, double_width)
    outgoing = jnp.concatenate(
        [
            jnp.concatenate(
                [
                    picked[..., h * half_width : (h + 1) * half_width],
                    picked[..., width + h * half_width : width + (h + 1) * half_width],
                ],
                axis=-1,
            )
            for h in range(2)
        ],
        axis=1,
    ).reshape(2 * groups, piece_len, width)
    incoming = lax.all_to_all(outgoing, ("yh0",) + GROUP, 0, 0, tiled=True)
    pieces = incoming.reshape(2 * groups * piece_len, width)
    history = lax.all_gather(pieces, "z", tiled=True)

    queries = cand_query[0]
    own_half = lax.dynamic_slice_in_dim(queries, core * half_width, half_width, 1)
    other_half = lax.dynamic_slice_in_dim(queries, (1 - core) * half_width, half_width, 1)
    partner_half = swapped(other_half)
    first = jnp.where(core == 0, own_half, partner_half)
    second = jnp.where(core == 0, partner_half, own_half)
    spread = lax.all_to_all(jnp.stack([first, second, second, first]), Y, 0, 0, tiled=True)

    about = jnp.concatenate([buckets[0], lengths])
    about = jnp.where(core == side, about, swapped(about))
    session = (group_index // 2) * 2 + side
    own_holding = lax.dynamic_index_in_dim(holding, session, 0, keepdims=False)
    arrived = own_holding[None, :] == jnp.arange(groups, dtype=jnp.int32)[:, None]
    piece_of = jnp.sum(jnp.where(arrived, jnp.arange(slots, dtype=jnp.int32)[None, :], 0), axis=1)
    order = jnp.arange(z_size, dtype=jnp.int32)[:, None, None, None]
    order = order + (jnp.arange(2, dtype=jnp.int32)[None, :, None, None] + 2 * upper_y) * z_size
    place = (
        (order * slots + piece_of[None, None, :, None]) * piece_len
        + jnp.arange(piece_len, dtype=jnp.int32)[None, None, None, :]
    ).reshape(-1)
    mask = (place < about[-1]).astype(jnp.float32)[None, :]
    one_hot = (
        about[place][:, None] == jnp.arange(time_bias.shape[0], dtype=jnp.int32)[None, :]
    ).astype(jnp.float32)
    own_bias = lax.dynamic_slice_in_dim(time_bias, core * (HEADS // 2), HEADS // 2, 1)
    bias = 0.5 * jnp.einsum("kn,nh->hk", one_hot, own_bias, precision=lax.Precision.HIGHEST)

    base = own_term(queries, cand_kv[0], self_bias)
    bias, mask, base = lax.optimization_barrier((bias[:, None, :], mask, base))
    order = send_order()[lax.axis_index(Y + ("core",))]
    partial = attend(order, spread, history, bias, mask, 2)
    parts = [None] * 4
    for step in (3, 2, 1, 0):
        parts[step] = lax.ppermute(partial[step], Y + ("core",), send_pairs(step))
    flag = ((core == 0) == (core == side)).astype(jnp.int32)
    return finish(flag, parts, base, cand_gate[0], norm_gain)[None]


def solution(mesh):
    split = Mesh(mesh.devices.reshape(2, 2, 8, 4, 2, 2), LOOP + GROUP)
    rows = P(GROUP, LOOP, None)
    return jax.shard_map(
        per_device,
        mesh=split,
        in_specs=(
            rows,
            rows,
            rows,
            P(GROUP, LOOP, None, None),
            P(),
            P(GROUP),
            P(GROUP, None),
            P(),
            P(),
            P(),
        ),
        out_specs=rows,
        check_vma=False,
    )
```

```python
import math

import jax
import jax.numpy as jnp
from jax import lax
from jax.experimental import pallas as pl
from jax.experimental.pallas import tpu as pltpu
from jax.sharding import Mesh
from jax.sharding import PartitionSpec as P

HEADS = 16
HEAD_DIM = 128
GROUP = ("x", "ylo", "core")
LOOP = ("yh1", "yh0", "z")
Y = ("yh1", "yh0")


HOMES = {(0, 0): (1, 3, 2, 0), (0, 1): (0, 1, 3, 2), (3, 0): (2, 0, 1, 3), (3, 1): (3, 2, 0, 1)}


def send_pairs(step):
    pairs = []
    for (yhi, core), homes in HOMES.items():
        pairs.append((yhi * 2 + core, homes[step] * 2))
        pairs.append(((yhi + 2) % 4 * 2 + 1 - core, (homes[step] + 2) % 4 * 2 + 1))
    return pairs


def make_attend_kernel(pieces, blocks, with_base):
    def kernel(*refs):
        q_refs, refs = refs[:blocks], refs[blocks:]
        k_refs, v_refs = refs[:pieces], refs[pieces : 2 * pieces]
        bias_ref, mask_ref = refs[2 * pieces : 2 * pieces + 2]
        base_refs = refs[2 * pieces + 2 : -blocks]
        out_refs = refs[-blocks:]
        rows = q_refs[0].shape[0]
        scale = 0.5 / math.sqrt(HEAD_DIM)
        inside = mask_ref[...] > 0.0
        for head in range(bias_ref.shape[0]):
            cols = slice(head * HEAD_DIM, (head + 1) * HEAD_DIM)
            queries = jnp.concatenate([q_ref[:, cols] for q_ref in q_refs], axis=0)
            keys = jnp.concatenate([k_ref[:, cols] for k_ref in k_refs], axis=0)
            values = jnp.concatenate([v_ref[:, cols] for v_ref in v_refs], axis=0)
            scores = lax.dot_general(
                queries, keys, (((1,), (1,)), ((), ())), preferred_element_type=jnp.float32
            )
            half = scores * scale + bias_ref[head]
            weights = jnp.where(inside, half + half * jnp.tanh(half), 0.0).astype(jnp.bfloat16)
            sums = jnp.dot(weights, values, preferred_element_type=jnp.float32)
            for i, out_ref in enumerate(out_refs):
                block = sums[i * rows : (i + 1) * rows]
                if with_base:
                    block = block + base_refs[i][:, cols]
                out_ref[:, cols] = block.astype(out_ref.dtype)

    return kernel


def attend(queries, history, bias, mask, per_step, out_type, base=()):
    blocks = len(queries)
    rows, full = queries[0].shape
    positions = mask.shape[1]
    width = per_step * HEAD_DIM
    steps = full // width
    spec = pl.BlockSpec((rows, width), lambda i: (0, i))
    return pl.pallas_call(
        make_attend_kernel(len(history), blocks, len(base) > 0),
        grid=(steps,),
        in_specs=[spec] * blocks
        + [pl.BlockSpec((h.shape[0], width), lambda i: (0, i)) for h in history]
        + [pl.BlockSpec((h.shape[0], width), lambda i: (0, i + steps)) for h in history]
        + [
            pl.BlockSpec((per_step, 1, positions), lambda i: (i, 0, 0)),
            pl.BlockSpec((1, positions), lambda i: (0, 0)),
        ]
        + [spec] * len(base),
        out_specs=[spec] * blocks,
        out_shape=[jax.ShapeDtypeStruct((rows, full), out_type)] * blocks,
        compiler_params=pltpu.CompilerParams(vmem_limit_bytes=56 * 1024 * 1024),
        cost_estimate=pl.CostEstimate(
            flops=4 * blocks * rows * positions * full,
            bytes_accessed=4 * positions * full + 4 * blocks * rows * full,
            transcendentals=blocks * rows * positions * full // HEAD_DIM,
        ),
    )(*queries, *history, *history, bias, mask, *base)


def shifted(value, axis, steps):
    count = lax.axis_size(axis)
    return lax.ppermute(value, axis, [(i, (i + steps) % count) for i in range(count)])


def own_kernel(q_ref, own_ref, self_bias_ref, out_ref):
    width = q_ref.shape[1]
    scale = 0.5 / math.sqrt(HEAD_DIM)
    for head in range(width // HEAD_DIM):
        cols = slice(head * HEAD_DIM, (head + 1) * HEAD_DIM)
        value_cols = slice(width + head * HEAD_DIM, width + (head + 1) * HEAD_DIM)
        product = q_ref[:, cols].astype(jnp.float32) * own_ref[:, cols].astype(jnp.float32)
        half = jnp.sum(product, axis=-1, keepdims=True) * scale + 0.5 * self_bias_ref[0, head]
        weight = (half + half * jnp.tanh(half)).astype(jnp.bfloat16).astype(jnp.float32)
        out_ref[:, cols] = weight * own_ref[:, value_cols].astype(jnp.float32)


def own_term(queries, own, self_bias):
    rows, width = queries.shape
    block = 32
    return pl.pallas_call(
        own_kernel,
        grid=(rows // block,),
        in_specs=[
            pl.BlockSpec((block, width), lambda i: (i, 0)),
            pl.BlockSpec((block, 2 * width), lambda i: (i, 0)),
            pl.BlockSpec(memory_space=pltpu.SMEM),
        ],
        out_specs=pl.BlockSpec((block, width), lambda i: (i, 0)),
        out_shape=jax.ShapeDtypeStruct((rows, width), jnp.float32),
    )(queries, own, self_bias[None])


def finish_kernel(flag_ref, a_ref, b_ref, c_ref, d_ref, base_ref, gate_ref, gain_ref, out_ref):
    a, b, c, d = (ref[...].astype(jnp.float32) for ref in (a_ref, b_ref, c_ref, d_ref))
    odd, even = a + c, b + d
    even_low = flag_ref[0] == 1
    low = jnp.where(even_low, even, odd)
    high = jnp.where(even_low, odd, even)
    total = base_ref[...] + jnp.concatenate([low, high], axis=-1)
    average = jnp.mean(total, axis=-1, keepdims=True)
    centered = total - average
    variance = jnp.mean(centered * centered, axis=-1, keepdims=True)
    normed = centered * lax.rsqrt(variance + 1e-05) * gain_ref[...]
    out_ref[...] = (normed * gate_ref[...].astype(jnp.float32)).astype(out_ref.dtype)


def finish(flag, parts, base, gate, gain):
    rows, width = gate.shape
    block = 64
    row_spec = lambda cols: pl.BlockSpec((block, cols), lambda i: (i, 0))
    return pl.pallas_call(
        finish_kernel,
        grid=(rows // block,),
        in_specs=[pl.BlockSpec(memory_space=pltpu.SMEM)]
        + [row_spec(width // 2)] * 4
        + [row_spec(width), row_spec(width), pl.BlockSpec((1, width), lambda i: (0, 0))],
        out_specs=row_spec(width),
        out_shape=jax.ShapeDtypeStruct((rows, width), jnp.bfloat16),
    )(flag[None], *parts, base, gate, gain[None])


def swapped(value):
    return lax.ppermute(value, "core", [(0, 1), (1, 0)])


def per_device(
    cand_query,
    cand_kv,
    cand_gate,
    cache_store,
    holders,
    lengths,
    buckets,
    time_bias,
    self_bias,
    norm_gain,
):
    core = lax.axis_index("core")
    upper_y = lax.axis_index("yh1")
    side = upper_y ^ lax.axis_index("yh0")
    group_index = lax.axis_index(GROUP)
    groups = lax.axis_size(GROUP)
    z_size = lax.axis_size("z")
    slots, _, piece_len, double_width = cache_store.shape
    width = double_width // 2
    half_width = width // 2

    holding = (holders // slots).reshape(groups, slots)
    slot_of = (holders % slots).reshape(groups, slots)
    chosen = jnp.sum(jnp.where(holding == group_index, slot_of, 0), axis=1).reshape(groups // 2, 2).T
    chosen = jnp.where(upper_y == 0, chosen, chosen[::-1]).reshape(-1)
    picked = cache_store[chosen, 0].reshape(groups, 1, piece_len, double_width)
    outgoing = jnp.concatenate(
        [
            jnp.concatenate(
                [
                    picked[..., h * half_width : (h + 1) * half_width],
                    picked[..., width + h * half_width : width + (h + 1) * half_width],
                ],
                axis=-1,
            )
            for h in range(2)
        ],
        axis=1,
    ).reshape(2 * groups, piece_len, width)
    incoming = lax.all_to_all(outgoing, ("yh0",) + GROUP, 0, 0, tiled=True)
    pieces = incoming.reshape(2 * groups * piece_len, width)
    history = [pieces]
    up = down = pieces
    for _ in range(3):
        up, down = shifted(up, "z", 1), shifted(down, "z", -1)
        history += [up, down]
    middle = pieces.shape[0] // 2
    last = [shifted(up[:middle], "z", 1), shifted(down[middle:], "z", -1)]

    flag = (core == 0) == (core == side)
    queries = cand_query[0]
    low, high = queries[:, :half_width], queries[:, half_width:]
    odd, even = jnp.where(flag, high, low), jnp.where(flag, low, high)
    spread = [
        lax.ppermute(half, Y + ("core",), [(home, worker) for worker, home in send_pairs(step)])
        for step, half in enumerate((odd, even, odd, even))
    ]

    about = jnp.concatenate([buckets[0], lengths])
    about = jnp.where(core == side, about, swapped(about))
    session = (group_index // 2) * 2 + side
    own_holding = lax.dynamic_index_in_dim(holding, session, 0, keepdims=False)
    arrived = own_holding[None, :] == jnp.arange(groups, dtype=jnp.int32)[:, None]
    piece_of = jnp.sum(jnp.where(arrived, jnp.arange(slots, dtype=jnp.int32)[None, :], 0), axis=1)
    order = (lax.axis_index("z") - jnp.array([0, 1, -1, 2, -2, 3, -3, 4], jnp.int32)) % z_size
    order = order[:, None, None, None]
    order = order + (jnp.arange(2, dtype=jnp.int32)[None, :, None, None] + 2 * upper_y) * z_size
    place = (
        (order * slots + piece_of[None, None, :, None]) * piece_len
        + jnp.arange(piece_len, dtype=jnp.int32)[None, None, None, :]
    ).reshape(-1)
    mask = (place < about[-1]).astype(jnp.float32)[None, :]
    one_hot = (
        about[place][:, None] == jnp.arange(time_bias.shape[0], dtype=jnp.int32)[None, :]
    ).astype(jnp.float32)
    own_bias = lax.dynamic_slice_in_dim(time_bias, core * (HEADS // 2), HEADS // 2, 1)
    bias = 0.5 * jnp.einsum("kn,nh->hk", one_hot, own_bias, precision=lax.Precision.HIGHEST)

    base = own_term(queries, cand_kv[0], self_bias)
    bias, mask, base = lax.optimization_barrier((bias[:, None, :], mask, base))
    cut = pieces.shape[0] * len(history)
    sums = attend(spread, history, bias[..., :cut], mask[:, :cut], 2, jnp.float32)
    partial = attend(spread, last, bias[..., cut:], mask[:, cut:], 4, jnp.bfloat16, sums)
    parts = [lax.ppermute(partial[s], Y + ("core",), send_pairs(s)) for s in range(4)]
    return finish(flag.astype(jnp.int32), parts, base, cand_gate[0], norm_gain)[None]


def solution(mesh):
    split = Mesh(mesh.devices.reshape(2, 2, 8, 4, 2, 2), LOOP + GROUP)
    rows = P(GROUP, LOOP, None)
    return jax.shard_map(
        per_device,
        mesh=split,
        in_specs=(
            rows,
            rows,
            rows,
            P(GROUP, LOOP, None, None),
            P(),
            P(GROUP),
            P(GROUP, None),
            P(),
            P(),
            P(),
        ),
        out_specs=rows,
        check_vma=False,
    )
```

```python
import math

import jax
import jax.numpy as jnp
from jax import lax
from jax.experimental import pallas as pl
from jax.experimental.pallas import tpu as pltpu
from jax.sharding import Mesh
from jax.sharding import PartitionSpec as P

HEADS = 16
HEAD_DIM = 128
VMEM = 62 * 1024 * 1024
GROUP = ("x", "ylo", "core")
LOOP = ("yh1", "yh0", "z")
Y = ("yh1", "yh0")


HOMES = {(0, 0): (1, 3, 2, 0), (0, 1): (0, 1, 3, 2), (3, 0): (2, 0, 1, 3), (3, 1): (3, 2, 0, 1)}


def send_pairs(step):
    pairs = []
    for (yhi, core), homes in HOMES.items():
        pairs.append((yhi * 2 + core, homes[step] * 2))
        pairs.append(((yhi + 2) % 4 * 2 + 1 - core, (homes[step] + 2) % 4 * 2 + 1))
    return pairs


def make_attend_kernel(pieces, blocks, with_base):
    def kernel(*refs):
        q_refs, refs = refs[:blocks], refs[blocks:]
        k_refs, v_refs = refs[:pieces], refs[pieces : 2 * pieces]
        bias_ref, mask_ref = refs[2 * pieces : 2 * pieces + 2]
        base_refs = refs[2 * pieces + 2 : -blocks]
        out_refs = refs[-blocks:]
        rows = q_refs[0].shape[0]
        scale = 0.5 / math.sqrt(HEAD_DIM)
        inside = mask_ref[...] > 0.0
        for head in range(bias_ref.shape[0]):
            cols = slice(head * HEAD_DIM, (head + 1) * HEAD_DIM)
            queries = jnp.concatenate([q_ref[:, cols] for q_ref in q_refs], axis=0)
            keys = jnp.concatenate([k_ref[:, cols] for k_ref in k_refs], axis=0)
            values = jnp.concatenate([v_ref[:, cols] for v_ref in v_refs], axis=0)
            scores = lax.dot_general(
                queries, keys, (((1,), (1,)), ((), ())), preferred_element_type=jnp.float32
            )
            half = scores * scale + bias_ref[head]
            weights = jnp.where(inside, half + half * jnp.tanh(half), 0.0).astype(jnp.bfloat16)
            sums = jnp.dot(weights, values, preferred_element_type=jnp.float32)
            for i, out_ref in enumerate(out_refs):
                block = sums[i * rows : (i + 1) * rows]
                if with_base:
                    block = block + base_refs[i][:, cols]
                out_ref[:, cols] = block.astype(out_ref.dtype)

    return kernel


def attend(queries, history, bias, mask, per_step, out_type, base=()):
    blocks = len(queries)
    rows, full = queries[0].shape
    positions = mask.shape[1]
    width = per_step * HEAD_DIM
    steps = full // width
    spec = pl.BlockSpec((rows, width), lambda i: (0, i))
    return pl.pallas_call(
        make_attend_kernel(len(history), blocks, len(base) > 0),
        grid=(steps,),
        in_specs=[spec] * blocks
        + [pl.BlockSpec((h.shape[0], width), lambda i: (0, i)) for h in history]
        + [pl.BlockSpec((h.shape[0], width), lambda i: (0, i + steps)) for h in history]
        + [
            pl.BlockSpec((per_step, 1, positions), lambda i: (i, 0, 0)),
            pl.BlockSpec((1, positions), lambda i: (0, 0)),
        ]
        + [spec] * len(base),
        out_specs=[spec] * blocks,
        out_shape=[jax.ShapeDtypeStruct((rows, full), out_type)] * blocks,
        compiler_params=pltpu.CompilerParams(vmem_limit_bytes=VMEM),
        cost_estimate=pl.CostEstimate(
            flops=4 * blocks * rows * positions * full,
            bytes_accessed=4 * positions * full + 4 * blocks * rows * full,
            transcendentals=blocks * rows * positions * full // HEAD_DIM,
        ),
    )(*queries, *history, *history, bias, mask, *base)


def shifted(value, axis, steps):
    count = lax.axis_size(axis)
    return lax.ppermute(value, axis, [(i, (i + steps) % count) for i in range(count)])


def own_kernel(q_ref, own_ref, self_bias_ref, out_ref):
    width = q_ref.shape[1]
    scale = 0.5 / math.sqrt(HEAD_DIM)
    for head in range(width // HEAD_DIM):
        cols = slice(head * HEAD_DIM, (head + 1) * HEAD_DIM)
        value_cols = slice(width + head * HEAD_DIM, width + (head + 1) * HEAD_DIM)
        product = q_ref[:, cols].astype(jnp.float32) * own_ref[:, cols].astype(jnp.float32)
        half = jnp.sum(product, axis=-1, keepdims=True) * scale + 0.5 * self_bias_ref[0, head]
        weight = (half + half * jnp.tanh(half)).astype(jnp.bfloat16).astype(jnp.float32)
        out_ref[:, cols] = weight * own_ref[:, value_cols].astype(jnp.float32)


def own_term(queries, own, self_bias):
    rows, width = queries.shape
    block = 32
    return pl.pallas_call(
        own_kernel,
        grid=(rows // block,),
        in_specs=[
            pl.BlockSpec((block, width), lambda i: (i, 0)),
            pl.BlockSpec((block, 2 * width), lambda i: (i, 0)),
            pl.BlockSpec(memory_space=pltpu.SMEM),
        ],
        out_specs=pl.BlockSpec((block, width), lambda i: (i, 0)),
        out_shape=jax.ShapeDtypeStruct((rows, width), jnp.float32),
        compiler_params=pltpu.CompilerParams(vmem_limit_bytes=VMEM),
    )(queries, own, self_bias[None])


def finish_kernel(flag_ref, d_ref, c_ref, b_ref, a_ref, base_ref, gate_ref, gain_ref, out_ref):
    a, b, c, d = (ref[...].astype(jnp.float32) for ref in (a_ref, b_ref, c_ref, d_ref))
    odd, even = a + c, b + d
    even_low = flag_ref[0] == 1
    low = jnp.where(even_low, even, odd)
    high = jnp.where(even_low, odd, even)
    total = base_ref[...] + jnp.concatenate([low, high], axis=-1)
    average = jnp.mean(total, axis=-1, keepdims=True)
    centered = total - average
    variance = jnp.mean(centered * centered, axis=-1, keepdims=True)
    normed = centered * lax.rsqrt(variance + 1e-05) * gain_ref[...]
    out_ref[...] = (normed * gate_ref[...].astype(jnp.float32)).astype(out_ref.dtype)


def finish(flag, parts, base, gate, gain):
    rows, width = gate.shape
    block = 64
    row_spec = lambda cols: pl.BlockSpec((block, cols), lambda i: (i, 0))
    return pl.pallas_call(
        finish_kernel,
        grid=(rows // block,),
        in_specs=[pl.BlockSpec(memory_space=pltpu.SMEM)]
        + [row_spec(width // 2)] * 4
        + [row_spec(width), row_spec(width), pl.BlockSpec((1, width), lambda i: (0, 0))],
        out_specs=row_spec(width),
        out_shape=jax.ShapeDtypeStruct((rows, width), jnp.bfloat16),
        compiler_params=pltpu.CompilerParams(vmem_limit_bytes=VMEM),
    )(flag[None], *parts[::-1], base, gate, gain[None])


def swapped(value):
    return lax.ppermute(value, "core", [(0, 1), (1, 0)])


def per_device(
    cand_query,
    cand_kv,
    cand_gate,
    cache_store,
    holders,
    lengths,
    buckets,
    time_bias,
    self_bias,
    norm_gain,
):
    core = lax.axis_index("core")
    upper_y = lax.axis_index("yh1")
    side = upper_y ^ lax.axis_index("yh0")
    group_index = lax.axis_index(GROUP)
    groups = lax.axis_size(GROUP)
    z_size = lax.axis_size("z")
    slots, _, piece_len, double_width = cache_store.shape
    width = double_width // 2
    half_width = width // 2

    holding = (holders // slots).reshape(groups, slots)
    slot_of = (holders % slots).reshape(groups, slots)
    chosen = jnp.sum(jnp.where(holding == group_index, slot_of, 0), axis=1).reshape(groups // 2, 2).T
    chosen = jnp.where(upper_y == 0, chosen, chosen[::-1]).reshape(-1)
    picked = cache_store[chosen, 0].reshape(groups, 1, piece_len, double_width)
    outgoing = jnp.concatenate(
        [
            jnp.concatenate(
                [
                    picked[..., h * half_width : (h + 1) * half_width],
                    picked[..., width + h * half_width : width + (h + 1) * half_width],
                ],
                axis=-1,
            )
            for h in range(2)
        ],
        axis=1,
    ).reshape(2 * groups, piece_len, width)
    incoming = lax.all_to_all(outgoing, ("yh0",) + GROUP, 0, 0, tiled=True)
    pieces = incoming.reshape(2 * groups * piece_len, width)
    flag = (core == 0) == (core == side)
    queries = cand_query[0]
    low, high = queries[:, :half_width], queries[:, half_width:]
    odd, even = jnp.where(flag, high, low), jnp.where(flag, low, high)
    spread = [
        lax.ppermute(half, Y + ("core",), [(home, worker) for worker, home in send_pairs(step)])
        for step, half in enumerate((odd, even, odd, even))
    ]

    about = jnp.concatenate([buckets[0], lengths])
    about = jnp.where(core == side, about, swapped(about))
    session = (group_index // 2) * 2 + side
    own_holding = lax.dynamic_index_in_dim(holding, session, 0, keepdims=False)
    arrived = own_holding[None, :] == jnp.arange(groups, dtype=jnp.int32)[:, None]
    piece_of = jnp.sum(jnp.where(arrived, jnp.arange(slots, dtype=jnp.int32)[None, :], 0), axis=1)
    near = (lax.axis_index("z") - jnp.array([0, 1, -1, 2, -2, 3, -3, 4], jnp.int32)) % z_size
    near_hot = (near[:, None] == jnp.arange(z_size, dtype=jnp.int32)[None, :]).astype(jnp.float32)
    half_rows = about.shape[0] // 2
    rows = lax.dynamic_slice_in_dim(about[:-1], upper_y * half_rows, half_rows).astype(jnp.float32)
    rows = rows.reshape(2, z_size, slots, piece_len)
    rows = jnp.einsum("sj,yzjr->yzsr", arrived.astype(jnp.float32), rows, precision=lax.Precision.HIGHEST)
    rows = jnp.einsum("nz,yzsr->nysr", near_hot, rows, precision=lax.Precision.HIGHEST)
    order = near[:, None, None, None] + z_size * (
        2 * upper_y + jnp.arange(2, dtype=jnp.int32)[None, :, None, None]
    )
    place = (order * slots + piece_of[None, None, :, None]) * piece_len
    place = place + jnp.arange(piece_len, dtype=jnp.int32)[None, None, None, :]
    own_bias = 0.5 * lax.dynamic_slice_in_dim(time_bias, core * (HEADS // 2), HEADS // 2, 1)

    def bias_and_mask(part):
        numbers = rows[part].reshape(-1, 1)
        table = jnp.arange(time_bias.shape[0], dtype=jnp.int32).astype(jnp.float32)
        one_hot = (jnp.abs(numbers - table[None, :]) < 0.5).astype(jnp.float32)
        bias = jnp.einsum("kn,nh->hk", one_hot, own_bias, precision=lax.Precision.HIGHEST)
        return bias[:, None, :], (place[part].reshape(1, -1) < about[-1]).astype(jnp.float32)

    first = bias_and_mask(slice(0, 7))
    second = bias_and_mask(slice(7, 8))
    base = own_term(queries, cand_kv[0], self_bias)
    pieces, base, first, second, spread[2], spread[3] = lax.optimization_barrier(
        (pieces, base, first, second, spread[2], spread[3])
    )

    history = [pieces]
    up = down = pieces
    for step in range(3):
        if step == 2:
            up, down, spread[0], spread[1] = lax.optimization_barrier((up, down, spread[0], spread[1]))
        up, down = shifted(up, "z", 1), shifted(down, "z", -1)
        history += [up, down]
    middle = pieces.shape[0] // 2
    last = [shifted(up[:middle], "z", 1), shifted(down[middle:], "z", -1)]

    sums = attend(spread, history, *first, 2, jnp.float32)
    partial = attend(spread, last, *second, 4, jnp.bfloat16, sums)
    parts = [lax.ppermute(partial[s], Y + ("core",), send_pairs(s)) for s in range(4)]
    return finish(flag.astype(jnp.int32), parts, base, cand_gate[0], norm_gain)[None]


def solution(mesh):
    split = Mesh(mesh.devices.reshape(2, 2, 8, 4, 2, 2), LOOP + GROUP)
    rows = P(GROUP, LOOP, None)
    return jax.shard_map(
        per_device,
        mesh=split,
        in_specs=(
            rows,
            rows,
            rows,
            P(GROUP, LOOP, None, None),
            P(),
            P(GROUP),
            P(GROUP, None),
            P(),
            P(),
            P(),
        ),
        out_specs=rows,
        check_vma=False,
    )
```

```python
import math

import jax
import jax.numpy as jnp
from jax import lax
from jax.experimental import pallas as pl
from jax.experimental.pallas import tpu as pltpu
from jax.sharding import Mesh
from jax.sharding import PartitionSpec as P

HEADS = 16
HEAD_DIM = 128
GROUP = ("x", "ylo", "core")
LOOP = ("yh1", "yh0", "z")
Y = ("yh1", "yh0")


HOMES = {(0, 0): (1, 3, 2, 0), (0, 1): (0, 1, 3, 2), (3, 0): (2, 0, 1, 3), (3, 1): (3, 2, 0, 1)}


def send_pairs(step):
    pairs = []
    for (yhi, core), homes in HOMES.items():
        pairs.append((yhi * 2 + core, homes[step] * 2))
        pairs.append(((yhi + 2) % 4 * 2 + 1 - core, (homes[step] + 2) % 4 * 2 + 1))
    return pairs


def send_order():
    order = [None] * 8
    for (yhi, core), homes in HOMES.items():
        order[yhi * 2 + core] = list(homes)
        order[(yhi + 2) % 4 * 2 + 1 - core] = [(home + 2) % 4 for home in homes]
    return jnp.array(order, jnp.int32)


def make_attend_kernel(blocks, with_base):
    def kernel(order_ref, q_ref, k_ref, v_ref, bias_ref, mask_ref, *refs):
        base_refs, out_refs = refs[:-blocks], refs[-blocks:]
        rows = q_ref.shape[1]
        scale = 0.5 / math.sqrt(HEAD_DIM)
        inside = mask_ref[...] > 0.0
        for head in range(bias_ref.shape[0]):
            cols = slice(head * HEAD_DIM, (head + 1) * HEAD_DIM)
            queries = jnp.concatenate([q_ref[order_ref[i], :, cols] for i in range(blocks)], axis=0)
            scores = lax.dot_general(
                queries,
                k_ref[:, cols],
                (((1,), (1,)), ((), ())),
                preferred_element_type=jnp.float32,
            )
            half = scores * scale + bias_ref[head]
            weights = jnp.where(inside, half + half * jnp.tanh(half), 0.0).astype(jnp.bfloat16)
            sums = jnp.dot(weights, v_ref[:, cols], preferred_element_type=jnp.float32)
            for i, out_ref in enumerate(out_refs):
                block = sums[i * rows : (i + 1) * rows]
                if with_base:
                    block = block + base_refs[i][:, cols]
                out_ref[:, cols] = block.astype(out_ref.dtype)

    return kernel


def attend(order, queries, history, bias, mask, per_step, out_type, base=()):
    blocks, rows, full = queries.shape
    positions = history.shape[0]
    width = per_step * HEAD_DIM
    steps = full // width
    spec = pl.BlockSpec((rows, width), lambda i: (0, i))
    return pl.pallas_call(
        make_attend_kernel(blocks, len(base) > 0),
        grid=(steps,),
        in_specs=[
            pl.BlockSpec(memory_space=pltpu.SMEM),
            pl.BlockSpec((blocks, rows, width), lambda i: (0, 0, i)),
            pl.BlockSpec((positions, width), lambda i: (0, i)),
            pl.BlockSpec((positions, width), lambda i: (0, i + steps)),
            pl.BlockSpec((per_step, 1, positions), lambda i: (i, 0, 0)),
            pl.BlockSpec((1, positions), lambda i: (0, 0)),
        ]
        + [spec] * len(base),
        out_specs=[spec] * blocks,
        out_shape=[jax.ShapeDtypeStruct((rows, full), out_type)] * blocks,
        compiler_params=pltpu.CompilerParams(vmem_limit_bytes=56 * 1024 * 1024),
        cost_estimate=pl.CostEstimate(
            flops=4 * blocks * rows * positions * full,
            bytes_accessed=4 * positions * full + 4 * blocks * rows * full,
            transcendentals=blocks * rows * positions * full // HEAD_DIM,
        ),
    )(order, queries, history, history, bias, mask, *base)


def own_kernel(q_ref, own_ref, self_bias_ref, out_ref):
    width = q_ref.shape[1]
    scale = 0.5 / math.sqrt(HEAD_DIM)
    for head in range(width // HEAD_DIM):
        cols = slice(head * HEAD_DIM, (head + 1) * HEAD_DIM)
        value_cols = slice(width + head * HEAD_DIM, width + (head + 1) * HEAD_DIM)
        product = q_ref[:, cols].astype(jnp.float32) * own_ref[:, cols].astype(jnp.float32)
        half = jnp.sum(product, axis=-1, keepdims=True) * scale + 0.5 * self_bias_ref[0, head]
        weight = (half + half * jnp.tanh(half)).astype(jnp.bfloat16).astype(jnp.float32)
        out_ref[:, cols] = weight * own_ref[:, value_cols].astype(jnp.float32)


def own_term(queries, own, self_bias):
    rows, width = queries.shape
    block = 32
    return pl.pallas_call(
        own_kernel,
        grid=(rows // block,),
        in_specs=[
            pl.BlockSpec((block, width), lambda i: (i, 0)),
            pl.BlockSpec((block, 2 * width), lambda i: (i, 0)),
            pl.BlockSpec(memory_space=pltpu.SMEM),
        ],
        out_specs=pl.BlockSpec((block, width), lambda i: (i, 0)),
        out_shape=jax.ShapeDtypeStruct((rows, width), jnp.float32),
    )(queries, own, self_bias[None])


def finish_kernel(flag_ref, d_ref, c_ref, b_ref, a_ref, base_ref, gate_ref, gain_ref, out_ref):
    a, b, c, d = (ref[...].astype(jnp.float32) for ref in (a_ref, b_ref, c_ref, d_ref))
    odd, even = a + c, b + d
    even_low = flag_ref[0] == 1
    low = jnp.where(even_low, even, odd)
    high = jnp.where(even_low, odd, even)
    total = base_ref[...] + jnp.concatenate([low, high], axis=-1)
    average = jnp.mean(total, axis=-1, keepdims=True)
    centered = total - average
    variance = jnp.mean(centered * centered, axis=-1, keepdims=True)
    normed = centered * lax.rsqrt(variance + 1e-05) * gain_ref[...]
    out_ref[...] = (normed * gate_ref[...].astype(jnp.float32)).astype(out_ref.dtype)


def finish(flag, parts, base, gate, gain):
    rows, width = gate.shape
    block = 64
    row_spec = lambda cols: pl.BlockSpec((block, cols), lambda i: (i, 0))
    return pl.pallas_call(
        finish_kernel,
        grid=(rows // block,),
        in_specs=[pl.BlockSpec(memory_space=pltpu.SMEM)]
        + [row_spec(width // 2)] * 4
        + [row_spec(width), row_spec(width), pl.BlockSpec((1, width), lambda i: (0, 0))],
        out_specs=row_spec(width),
        out_shape=jax.ShapeDtypeStruct((rows, width), jnp.bfloat16),
        compiler_params=pltpu.CompilerParams(vmem_limit_bytes=12 * 1024 * 1024),
    )(flag[None], *parts[::-1], base, gate, gain[None])


def swapped(value):
    return lax.ppermute(value, "core", [(0, 1), (1, 0)])


def per_device(
    cand_query,
    cand_kv,
    cand_gate,
    cache_store,
    holders,
    lengths,
    buckets,
    time_bias,
    self_bias,
    norm_gain,
):
    core = lax.axis_index("core")
    upper_y = lax.axis_index("yh1")
    side = upper_y ^ lax.axis_index("yh0")
    group_index = lax.axis_index(GROUP)
    groups = lax.axis_size(GROUP)
    z_size = lax.axis_size("z")
    slots, _, piece_len, double_width = cache_store.shape
    width = double_width // 2
    half_width = width // 2

    holding = (holders // slots).reshape(groups, slots)
    slot_of = (holders % slots).reshape(groups, slots)
    chosen = jnp.sum(jnp.where(holding == group_index, slot_of, 0), axis=1).reshape(groups // 2, 2).T
    chosen = jnp.where(upper_y == 0, chosen, chosen[::-1]).reshape(-1)
    picked = cache_store[chosen, 0].reshape(groups, 1, piece_len, double_width)
    outgoing = jnp.concatenate(
        [
            jnp.concatenate(
                [
                    picked[..., h * half_width : (h + 1) * half_width],
                    picked[..., width + h * half_width : width + (h + 1) * half_width],
                ],
                axis=-1,
            )
            for h in range(2)
        ],
        axis=1,
    ).reshape(2 * groups, piece_len, width)
    incoming = lax.all_to_all(outgoing, ("yh0",) + GROUP, 0, 0, tiled=True)
    pieces = incoming.reshape(2 * groups * piece_len, width)
    early = 16
    history = lax.all_gather(pieces[early:], "z", tiled=True)

    queries = cand_query[0]
    own_half = lax.dynamic_slice_in_dim(queries, core * half_width, half_width, 1)
    other_half = lax.dynamic_slice_in_dim(queries, (1 - core) * half_width, half_width, 1)
    partner_half = swapped(other_half)
    first = jnp.where(core == 0, own_half, partner_half)
    second = jnp.where(core == 0, partner_half, own_half)
    spread = lax.all_to_all(jnp.stack([first, second, second, first]), Y, 0, 0, tiled=True)

    about = jnp.concatenate([buckets[0], lengths])
    about = jnp.where(core == side, about, swapped(about))
    session = (group_index // 2) * 2 + side
    own_holding = lax.dynamic_index_in_dim(holding, session, 0, keepdims=False)
    arrived = own_holding[None, :] == jnp.arange(groups, dtype=jnp.int32)[:, None]
    piece_of = jnp.sum(jnp.where(arrived, jnp.arange(slots, dtype=jnp.int32)[None, :], 0), axis=1)
    half_rows = about.shape[0] // 2
    rows = lax.dynamic_slice_in_dim(about[:-1], upper_y * half_rows, half_rows).astype(jnp.float32)
    rows = rows.reshape(2, z_size, slots, piece_len)
    rows = jnp.einsum("sj,yzjr->zysr", arrived.astype(jnp.float32), rows, precision=lax.Precision.HIGHEST)
    rows = rows.reshape(z_size, -1)
    loop = jnp.arange(z_size, dtype=jnp.int32)[:, None, None, None]
    loop = loop + z_size * (2 * upper_y + jnp.arange(2, dtype=jnp.int32)[None, :, None, None])
    place = (loop * slots + piece_of[None, None, :, None]) * piece_len
    place = (place + jnp.arange(piece_len, dtype=jnp.int32)[None, None, None, :]).reshape(z_size, -1)
    own_bias = 0.5 * lax.dynamic_slice_in_dim(time_bias, core * (HEADS // 2), HEADS // 2, 1)

    def bias_and_mask(part):
        numbers = rows[:, part].reshape(-1, 1)
        table = jnp.arange(time_bias.shape[0], dtype=jnp.int32).astype(jnp.float32)
        one_hot = (jnp.abs(numbers - table[None, :]) < 0.5).astype(jnp.float32)
        bias = jnp.einsum("kn,nh->hk", one_hot, own_bias, precision=lax.Precision.HIGHEST)
        return bias[:, None, :], (place[:, part].reshape(1, -1) < about[-1]).astype(jnp.float32)

    first = bias_and_mask(slice(0, early))
    second = bias_and_mask(slice(early, None))
    base = own_term(queries, cand_kv[0], self_bias)
    order = send_order()[lax.axis_index(Y + ("core",))]
    start, base, first, second, order = lax.optimization_barrier(
        (pieces[:early], base, first, second, order)
    )
    early_history = lax.all_gather(start, "z", tiled=True)
    sums = attend(order, spread, early_history, *first, 4, jnp.float32)
    partial = attend(order, spread, history, *second, 2, jnp.bfloat16, sums)
    parts = [lax.ppermute(partial[s], Y + ("core",), send_pairs(s)) for s in range(4)]
    flag = ((core == 0) == (core == side)).astype(jnp.int32)
    return finish(flag, parts, base, cand_gate[0], norm_gain)[None]


def solution(mesh):
    split = Mesh(mesh.devices.reshape(2, 2, 8, 4, 2, 2), LOOP + GROUP)
    rows = P(GROUP, LOOP, None)
    return jax.shard_map(
        per_device,
        mesh=split,
        in_specs=(
            rows,
            rows,
            rows,
            P(GROUP, LOOP, None, None),
            P(),
            P(GROUP),
            P(GROUP, None),
            P(),
            P(),
            P(),
        ),
        out_specs=rows,
        check_vma=False,
    )
```

```python
import math

import jax
import jax.numpy as jnp
from jax import lax
from jax.experimental import pallas as pl
from jax.experimental.pallas import tpu as pltpu
from jax.sharding import Mesh
from jax.sharding import PartitionSpec as P

HEADS = 16
HEAD_DIM = 128
PER_STEP = 4
GROUP = ("x", "ylo", "core")
LOOP = ("yh1", "yh0", "z")
Y = ("yh1", "yh0")


HOMES = {(0, 0): (1, 3, 2, 0), (0, 1): (0, 1, 3, 2), (3, 0): (2, 0, 1, 3), (3, 1): (3, 2, 0, 1)}


def send_pairs(step):
    pairs = []
    for (yhi, core), homes in HOMES.items():
        pairs.append((yhi * 2 + core, homes[step] * 2))
        pairs.append(((yhi + 2) % 4 * 2 + 1 - core, (homes[step] + 2) % 4 * 2 + 1))
    return pairs


def send_order():
    order = [None] * 8
    for (yhi, core), homes in HOMES.items():
        order[yhi * 2 + core] = list(homes)
        order[(yhi + 2) % 4 * 2 + 1 - core] = [(home + 2) % 4 for home in homes]
    return jnp.array(order, jnp.int32)


def attend_kernel(order_ref, q_ref, k_ref, v_ref, bias_ref, mask_ref, *out_refs):
    rows = q_ref.shape[1]
    scale = 0.5 / math.sqrt(HEAD_DIM)
    inside = mask_ref[...] > 0.0
    for head in range(bias_ref.shape[0]):
        cols = slice(head * HEAD_DIM, (head + 1) * HEAD_DIM)
        queries = jnp.concatenate(
            [q_ref[order_ref[i], :, cols] for i in range(len(out_refs))], axis=0
        )
        scores = lax.dot_general(
            queries, k_ref[:, cols], (((1,), (1,)), ((), ())), preferred_element_type=jnp.float32
        )
        half = scores * scale + bias_ref[head]
        weights = jnp.where(inside, half + half * jnp.tanh(half), 0.0).astype(jnp.bfloat16)
        sums = jnp.dot(weights, v_ref[:, cols], preferred_element_type=jnp.float32)
        for i, out_ref in enumerate(out_refs):
            out_ref[:, cols] = sums[i * rows : (i + 1) * rows].astype(out_ref.dtype)


def attend(order, queries, history, bias, mask, per_step):
    blocks, rows, full = queries.shape
    positions = history.shape[0]
    width = per_step * HEAD_DIM
    steps = full // width
    count = order.shape[0]
    return pl.pallas_call(
        attend_kernel,
        grid=(steps,),
        in_specs=[
            pl.BlockSpec(memory_space=pltpu.SMEM),
            pl.BlockSpec((blocks, rows, width), lambda i: (0, 0, i)),
            pl.BlockSpec((positions, width), lambda i: (0, i)),
            pl.BlockSpec((positions, width), lambda i: (0, i + steps)),
            pl.BlockSpec((per_step, 1, positions), lambda i: (i, 0, 0)),
            pl.BlockSpec((1, positions), lambda i: (0, 0)),
        ],
        out_specs=[pl.BlockSpec((rows, width), lambda i: (0, i))] * count,
        out_shape=[jax.ShapeDtypeStruct((rows, full), jnp.bfloat16)] * count,
        compiler_params=pltpu.CompilerParams(vmem_limit_bytes=56 * 1024 * 1024),
        cost_estimate=pl.CostEstimate(
            flops=4 * count * rows * positions * full,
            bytes_accessed=4 * positions * full + 4 * count * rows * full,
            transcendentals=count * rows * positions * full // HEAD_DIM,
        ),
    )(order, queries, history, history, bias, mask)


def own_kernel(q_ref, own_ref, self_bias_ref, out_ref):
    width = q_ref.shape[1]
    scale = 0.5 / math.sqrt(HEAD_DIM)
    for head in range(width // HEAD_DIM):
        cols = slice(head * HEAD_DIM, (head + 1) * HEAD_DIM)
        value_cols = slice(width + head * HEAD_DIM, width + (head + 1) * HEAD_DIM)
        product = q_ref[:, cols].astype(jnp.float32) * own_ref[:, cols].astype(jnp.float32)
        half = jnp.sum(product, axis=-1, keepdims=True) * scale + 0.5 * self_bias_ref[0, head]
        weight = (half + half * jnp.tanh(half)).astype(jnp.bfloat16).astype(jnp.float32)
        out_ref[:, cols] = weight * own_ref[:, value_cols].astype(jnp.float32)


def own_term(queries, own, self_bias):
    rows, width = queries.shape
    block = 32
    return pl.pallas_call(
        own_kernel,
        grid=(rows // block,),
        in_specs=[
            pl.BlockSpec((block, width), lambda i: (i, 0)),
            pl.BlockSpec((block, 2 * width), lambda i: (i, 0)),
            pl.BlockSpec(memory_space=pltpu.SMEM),
        ],
        out_specs=pl.BlockSpec((block, width), lambda i: (i, 0)),
        out_shape=jax.ShapeDtypeStruct((rows, width), jnp.float32),
    )(queries, own, self_bias[None])


def finish_kernel(flag_ref, d_ref, c_ref, b_ref, a_ref, base_ref, gate_ref, gain_ref, out_ref):
    a, b, c, d = (ref[...].astype(jnp.float32) for ref in (a_ref, b_ref, c_ref, d_ref))
    odd, even = a + c, b + d
    even_low = flag_ref[0] == 1
    low = jnp.where(even_low, even, odd)
    high = jnp.where(even_low, odd, even)
    total = base_ref[...] + jnp.concatenate([low, high], axis=-1)
    average = jnp.mean(total, axis=-1, keepdims=True)
    centered = total - average
    variance = jnp.mean(centered * centered, axis=-1, keepdims=True)
    normed = centered * lax.rsqrt(variance + 1e-05) * gain_ref[...]
    out_ref[...] = (normed * gate_ref[...].astype(jnp.float32)).astype(out_ref.dtype)


def finish(flag, parts, base, gate, gain):
    rows, width = gate.shape
    block = 64
    row_spec = lambda cols: pl.BlockSpec((block, cols), lambda i: (i, 0))
    return pl.pallas_call(
        finish_kernel,
        grid=(rows // block,),
        in_specs=[pl.BlockSpec(memory_space=pltpu.SMEM)]
        + [row_spec(width // 2)] * 4
        + [row_spec(width), row_spec(width), pl.BlockSpec((1, width), lambda i: (0, 0))],
        out_specs=row_spec(width),
        out_shape=jax.ShapeDtypeStruct((rows, width), jnp.bfloat16),
        compiler_params=pltpu.CompilerParams(vmem_limit_bytes=12 * 1024 * 1024),
    )(flag[None], *parts[::-1], base, gate, gain[None])


def swapped(value):
    return lax.ppermute(value, "core", [(0, 1), (1, 0)])


def per_device(
    cand_query,
    cand_kv,
    cand_gate,
    cache_store,
    holders,
    lengths,
    buckets,
    time_bias,
    self_bias,
    norm_gain,
):
    core = lax.axis_index("core")
    upper_y = lax.axis_index("yh1")
    side = upper_y ^ lax.axis_index("yh0")
    group_index = lax.axis_index(GROUP)
    groups = lax.axis_size(GROUP)
    z_size = lax.axis_size("z")
    slots, _, piece_len, double_width = cache_store.shape
    width = double_width // 2
    half_width = width // 2

    holding = (holders // slots).reshape(groups, slots)
    slot_of = (holders % slots).reshape(groups, slots)
    chosen = jnp.sum(jnp.where(holding == group_index, slot_of, 0), axis=1).reshape(groups // 2, 2).T
    chosen = jnp.where(upper_y == 0, chosen, chosen[::-1]).reshape(-1)
    picked = cache_store[chosen, 0].reshape(groups, 1, piece_len, double_width)
    outgoing = jnp.concatenate(
        [
            jnp.concatenate(
                [
                    picked[..., h * half_width : (h + 1) * half_width],
                    picked[..., width + h * half_width : width + (h + 1) * half_width],
                ],
                axis=-1,
            )
            for h in range(2)
        ],
        axis=1,
    ).reshape(2 * groups, piece_len, width)
    incoming = lax.all_to_all(outgoing, ("yh0",) + GROUP, 0, 0, tiled=True)
    pieces = incoming.reshape(2 * groups * piece_len, width)
    history = lax.all_gather(pieces, "z", tiled=True)

    queries = cand_query[0]
    own_half = lax.dynamic_slice_in_dim(queries, core * half_width, half_width, 1)
    other_half = lax.dynamic_slice_in_dim(queries, (1 - core) * half_width, half_width, 1)
    partner_half = swapped(other_half)
    first = jnp.where(core == 0, own_half, partner_half)
    second = jnp.where(core == 0, partner_half, own_half)
    spread = lax.all_to_all(jnp.stack([first, second, second, first]), Y, 0, 0, tiled=True)

    about = jnp.concatenate([buckets[0], lengths])
    about = jnp.where(core == side, about, swapped(about))
    session = (group_index // 2) * 2 + side
    own_holding = lax.dynamic_index_in_dim(holding, session, 0, keepdims=False)
    arrived = own_holding[None, :] == jnp.arange(groups, dtype=jnp.int32)[:, None]
    piece_of = jnp.sum(jnp.where(arrived, jnp.arange(slots, dtype=jnp.int32)[None, :], 0), axis=1)
    half_rows = about.shape[0] // 2
    rows = lax.dynamic_slice_in_dim(about[:-1], upper_y * half_rows, half_rows).astype(jnp.float32)
    rows = rows.reshape(2, z_size, slots, piece_len)
    rows = jnp.einsum("sj,yzjr->zysr", arrived.astype(jnp.float32), rows, precision=lax.Precision.HIGHEST)
    rows = rows.reshape(z_size, -1)
    loop = jnp.arange(z_size, dtype=jnp.int32)[:, None, None, None]
    loop = loop + z_size * (2 * upper_y + jnp.arange(2, dtype=jnp.int32)[None, :, None, None])
    place = (loop * slots + piece_of[None, None, :, None]) * piece_len
    place = (place + jnp.arange(piece_len, dtype=jnp.int32)[None, None, None, :]).reshape(z_size, -1)
    own_bias = 0.5 * lax.dynamic_slice_in_dim(time_bias, core * (HEADS // 2), HEADS // 2, 1)

    numbers = rows.reshape(-1, 1)
    table = jnp.arange(time_bias.shape[0], dtype=jnp.int32).astype(jnp.float32)
    one_hot = (jnp.abs(numbers - table[None, :]) < 0.5).astype(jnp.float32)
    bias = jnp.einsum("kn,nh->hk", one_hot, own_bias, precision=lax.Precision.HIGHEST)[:, None, :]
    mask = (place.reshape(1, -1) < about[-1]).astype(jnp.float32)
    base = own_term(queries, cand_kv[0], self_bias)
    order = send_order()[lax.axis_index(Y + ("core",))]
    bias, mask, base, order = lax.optimization_barrier((bias, mask, base, order))
    far = attend(order[2:], spread, history, bias, mask, PER_STEP)
    *far, rest = lax.optimization_barrier((*far, order[:2]))
    near = attend(rest, spread, history, bias, mask, PER_STEP)
    partial = [*near, *far]
    parts = [lax.ppermute(partial[s], Y + ("core",), send_pairs(s)) for s in range(4)]
    flag = ((core == 0) == (core == side)).astype(jnp.int32)
    return finish(flag, parts, base, cand_gate[0], norm_gain)[None]


def solution(mesh):
    split = Mesh(mesh.devices.reshape(2, 2, 8, 4, 2, 2), LOOP + GROUP)
    rows = P(GROUP, LOOP, None)
    return jax.shard_map(
        per_device,
        mesh=split,
        in_specs=(
            rows,
            rows,
            rows,
            P(GROUP, LOOP, None, None),
            P(),
            P(GROUP),
            P(GROUP, None),
            P(),
            P(),
            P(),
        ),
        out_specs=rows,
        check_vma=False,
    )
```

```python
import math

import jax
import jax.numpy as jnp
from jax import lax
from jax.experimental import pallas as pl
from jax.experimental.pallas import tpu as pltpu
from jax.sharding import Mesh
from jax.sharding import PartitionSpec as P

HEADS = 16
HEAD_DIM = 128
PER_STEP = 4
GROUP = ("x", "ylo", "core")
LOOP = ("yh1", "yh0", "z")
Y = ("yh1", "yh0")


HOMES = {(0, 0): (1, 3, 2, 0), (0, 1): (0, 1, 3, 2), (3, 0): (2, 0, 1, 3), (3, 1): (3, 2, 0, 1)}


def send_pairs(step):
    pairs = []
    for (yhi, core), homes in HOMES.items():
        pairs.append((yhi * 2 + core, homes[step] * 2))
        pairs.append(((yhi + 2) % 4 * 2 + 1 - core, (homes[step] + 2) % 4 * 2 + 1))
    return pairs


def send_order():
    order = [None] * 8
    for (yhi, core), homes in HOMES.items():
        order[yhi * 2 + core] = list(homes)
        order[(yhi + 2) % 4 * 2 + 1 - core] = [(home + 2) % 4 for home in homes]
    return jnp.array(order, jnp.int32)


def attend_kernel(order_ref, q_ref, k_ref, v_ref, bias_ref, mask_ref, *out_refs):
    rows = q_ref.shape[1]
    scale = 0.5 / math.sqrt(HEAD_DIM)
    inside = mask_ref[...] > 0.0
    for head in range(bias_ref.shape[0]):
        cols = slice(head * HEAD_DIM, (head + 1) * HEAD_DIM)
        queries = jnp.concatenate(
            [q_ref[order_ref[i], :, cols] for i in range(len(out_refs))], axis=0
        )
        scores = lax.dot_general(
            queries, k_ref[:, cols], (((1,), (1,)), ((), ())), preferred_element_type=jnp.float32
        )
        half = scores * scale + bias_ref[head]
        weights = jnp.where(inside, half + half * jnp.tanh(half), 0.0).astype(jnp.bfloat16)
        sums = jnp.dot(weights, v_ref[:, cols], preferred_element_type=jnp.float32)
        for i, out_ref in enumerate(out_refs):
            out_ref[:, cols] = sums[i * rows : (i + 1) * rows].astype(out_ref.dtype)


def attend(order, queries, history, bias, mask, per_step):
    blocks, rows, full = queries.shape
    positions = history.shape[0]
    width = per_step * HEAD_DIM
    steps = full // width
    count = order.shape[0]
    return pl.pallas_call(
        attend_kernel,
        grid=(steps,),
        in_specs=[
            pl.BlockSpec(memory_space=pltpu.SMEM),
            pl.BlockSpec((blocks, rows, width), lambda i: (0, 0, i)),
            pl.BlockSpec((positions, width), lambda i: (0, i)),
            pl.BlockSpec((positions, width), lambda i: (0, i + steps)),
            pl.BlockSpec((per_step, 1, positions), lambda i: (i, 0, 0)),
            pl.BlockSpec((1, positions), lambda i: (0, 0)),
        ],
        out_specs=[pl.BlockSpec((rows, width), lambda i: (0, i))] * count,
        out_shape=[jax.ShapeDtypeStruct((rows, full), jnp.bfloat16)] * count,
        compiler_params=pltpu.CompilerParams(vmem_limit_bytes=56 * 1024 * 1024),
        cost_estimate=pl.CostEstimate(
            flops=4 * count * rows * positions * full,
            bytes_accessed=4 * positions * full + 4 * count * rows * full,
            transcendentals=count * rows * positions * full // HEAD_DIM,
        ),
    )(order, queries, history, history, bias, mask)


def own_kernel(q_ref, own_ref, self_bias_ref, out_ref):
    width = q_ref.shape[1]
    scale = 0.5 / math.sqrt(HEAD_DIM)
    for head in range(width // HEAD_DIM):
        cols = slice(head * HEAD_DIM, (head + 1) * HEAD_DIM)
        value_cols = slice(width + head * HEAD_DIM, width + (head + 1) * HEAD_DIM)
        product = q_ref[:, cols].astype(jnp.float32) * own_ref[:, cols].astype(jnp.float32)
        half = jnp.sum(product, axis=-1, keepdims=True) * scale + 0.5 * self_bias_ref[0, head]
        weight = (half + half * jnp.tanh(half)).astype(jnp.bfloat16).astype(jnp.float32)
        out_ref[:, cols] = weight * own_ref[:, value_cols].astype(jnp.float32)


def own_term(queries, own, self_bias):
    rows, width = queries.shape
    block = 32
    return pl.pallas_call(
        own_kernel,
        grid=(rows // block,),
        in_specs=[
            pl.BlockSpec((block, width), lambda i: (i, 0)),
            pl.BlockSpec((block, 2 * width), lambda i: (i, 0)),
            pl.BlockSpec(memory_space=pltpu.SMEM),
        ],
        out_specs=pl.BlockSpec((block, width), lambda i: (i, 0)),
        out_shape=jax.ShapeDtypeStruct((rows, width), jnp.float32),
    )(queries, own, self_bias[None])


def finish_kernel(flag_ref, d_ref, c_ref, b_ref, a_ref, base_ref, gate_ref, gain_ref, out_ref):
    a, b, c, d = (ref[...].astype(jnp.float32) for ref in (a_ref, b_ref, c_ref, d_ref))
    odd, even = a + c, b + d
    even_low = flag_ref[0] == 1
    low = jnp.where(even_low, even, odd)
    high = jnp.where(even_low, odd, even)
    total = base_ref[...] + jnp.concatenate([low, high], axis=-1)
    average = jnp.mean(total, axis=-1, keepdims=True)
    centered = total - average
    variance = jnp.mean(centered * centered, axis=-1, keepdims=True)
    normed = centered * lax.rsqrt(variance + 1e-05) * gain_ref[...]
    out_ref[...] = (normed * gate_ref[...].astype(jnp.float32)).astype(out_ref.dtype)


def finish(flag, parts, base, gate, gain):
    rows, width = gate.shape
    block = 64
    row_spec = lambda cols: pl.BlockSpec((block, cols), lambda i: (i, 0))
    return pl.pallas_call(
        finish_kernel,
        grid=(rows // block,),
        in_specs=[pl.BlockSpec(memory_space=pltpu.SMEM)]
        + [row_spec(width // 2)] * 4
        + [row_spec(width), row_spec(width), pl.BlockSpec((1, width), lambda i: (0, 0))],
        out_specs=row_spec(width),
        out_shape=jax.ShapeDtypeStruct((rows, width), jnp.bfloat16),
        compiler_params=pltpu.CompilerParams(vmem_limit_bytes=12 * 1024 * 1024),
    )(flag[None], *parts[::-1], base, gate, gain[None])


def swapped(value):
    return lax.ppermute(value, "core", [(0, 1), (1, 0)])


def per_device(
    cand_query,
    cand_kv,
    cand_gate,
    cache_store,
    holders,
    lengths,
    buckets,
    time_bias,
    self_bias,
    norm_gain,
):
    core = lax.axis_index("core")
    upper_y = lax.axis_index("yh1")
    side = upper_y ^ lax.axis_index("yh0")
    group_index = lax.axis_index(GROUP)
    groups = lax.axis_size(GROUP)
    z_size = lax.axis_size("z")
    slots, _, piece_len, double_width = cache_store.shape
    width = double_width // 2
    half_width = width // 2

    holding = (holders // slots).reshape(groups, slots)
    slot_of = (holders % slots).reshape(groups, slots)
    chosen = jnp.sum(jnp.where(holding == group_index, slot_of, 0), axis=1).reshape(groups // 2, 2).T
    chosen = jnp.where(upper_y == 0, chosen, chosen[::-1]).reshape(-1)
    picked = cache_store[chosen, 0].reshape(groups, 1, piece_len, double_width)
    outgoing = jnp.concatenate(
        [
            jnp.concatenate(
                [
                    picked[..., h * half_width : (h + 1) * half_width],
                    picked[..., width + h * half_width : width + (h + 1) * half_width],
                ],
                axis=-1,
            )
            for h in range(2)
        ],
        axis=1,
    ).reshape(2 * groups, piece_len, width)
    incoming = lax.all_to_all(outgoing, ("yh0",) + GROUP, 0, 0, tiled=True)
    pieces = incoming.reshape(2 * groups * piece_len, width)
    history = lax.all_gather(pieces, "z", tiled=True)

    queries = cand_query[0]
    own_half = lax.dynamic_slice_in_dim(queries, core * half_width, half_width, 1)
    other_half = lax.dynamic_slice_in_dim(queries, (1 - core) * half_width, half_width, 1)
    partner_half = swapped(other_half)
    first = jnp.where(core == 0, own_half, partner_half)
    second = jnp.where(core == 0, partner_half, own_half)
    spread = lax.all_to_all(jnp.stack([first, second, second, first]), Y, 0, 0, tiled=True)

    about = jnp.concatenate([buckets[0], lengths])
    about = jnp.where(core == side, about, swapped(about))
    session = (group_index // 2) * 2 + side
    own_holding = lax.dynamic_index_in_dim(holding, session, 0, keepdims=False)
    arrived = own_holding[None, :] == jnp.arange(groups, dtype=jnp.int32)[:, None]
    piece_of = jnp.sum(jnp.where(arrived, jnp.arange(slots, dtype=jnp.int32)[None, :], 0), axis=1)
    half_rows = about.shape[0] // 2
    rows = lax.dynamic_slice_in_dim(about[:-1], upper_y * half_rows, half_rows).astype(jnp.float32)
    rows = rows.reshape(2, z_size, slots, piece_len)
    rows = jnp.einsum("sj,yzjr->zysr", arrived.astype(jnp.float32), rows, precision=lax.Precision.HIGHEST)
    rows = rows.reshape(z_size, -1)
    loop = jnp.arange(z_size, dtype=jnp.int32)[:, None, None, None]
    loop = loop + z_size * (2 * upper_y + jnp.arange(2, dtype=jnp.int32)[None, :, None, None])
    place = (loop * slots + piece_of[None, None, :, None]) * piece_len
    place = (place + jnp.arange(piece_len, dtype=jnp.int32)[None, None, None, :]).reshape(z_size, -1)
    own_bias = 0.5 * lax.dynamic_slice_in_dim(time_bias, core * (HEADS // 2), HEADS // 2, 1)

    numbers = rows.reshape(-1, 1)
    table = jnp.arange(time_bias.shape[0], dtype=jnp.int32).astype(jnp.float32)
    one_hot = (jnp.abs(numbers - table[None, :]) < 0.5).astype(jnp.float32)
    bias = jnp.einsum("kn,nh->hk", one_hot, own_bias, precision=lax.Precision.HIGHEST)[:, None, :]
    mask = (place.reshape(1, -1) < about[-1]).astype(jnp.float32)
    base = own_term(queries, cand_kv[0], self_bias)
    order = send_order()[lax.axis_index(Y + ("core",))]
    bias, mask, base, order = lax.optimization_barrier((bias, mask, base, order))
    (last,) = attend(order[3:], spread, history, bias, mask, PER_STEP)
    last, rest = lax.optimization_barrier((last, order[:3]))
    partial = [*attend(rest, spread, history, bias, mask, PER_STEP), last]
    parts = [lax.ppermute(partial[s], Y + ("core",), send_pairs(s)) for s in range(4)]
    flag = ((core == 0) == (core == side)).astype(jnp.int32)
    return finish(flag, parts, base, cand_gate[0], norm_gain)[None]


def solution(mesh):
    split = Mesh(mesh.devices.reshape(2, 2, 8, 4, 2, 2), LOOP + GROUP)
    rows = P(GROUP, LOOP, None)
    return jax.shard_map(
        per_device,
        mesh=split,
        in_specs=(
            rows,
            rows,
            rows,
            P(GROUP, LOOP, None, None),
            P(),
            P(GROUP),
            P(GROUP, None),
            P(),
            P(),
            P(),
        ),
        out_specs=rows,
        check_vma=False,
    )
```

```python
import math

import jax
import jax.numpy as jnp
from jax import lax
from jax.experimental import pallas as pl
from jax.experimental.pallas import tpu as pltpu
from jax.sharding import Mesh
from jax.sharding import PartitionSpec as P

HEADS = 16
HEAD_DIM = 128
PER_STEP = 4
GROUP = ("x", "ylo", "core")
LOOP = ("yh1", "yh0", "z")
Y = ("yh1", "yh0")


HOMES = {(0, 0): (1, 3, 2, 0), (0, 1): (0, 1, 3, 2), (3, 0): (2, 0, 1, 3), (3, 1): (3, 2, 0, 1)}


def send_pairs(step):
    pairs = []
    for (yhi, core), homes in HOMES.items():
        pairs.append((yhi * 2 + core, homes[step] * 2))
        pairs.append(((yhi + 2) % 4 * 2 + 1 - core, (homes[step] + 2) % 4 * 2 + 1))
    return pairs


def send_order():
    order = [None] * 8
    for (yhi, core), homes in HOMES.items():
        order[yhi * 2 + core] = list(homes)
        order[(yhi + 2) % 4 * 2 + 1 - core] = [(home + 2) % 4 for home in homes]
    return jnp.array(order, jnp.int32)


def attend_kernel(order_ref, q_ref, k_ref, v_ref, bias_ref, mask_ref, *out_refs):
    rows = q_ref.shape[1]
    scale = 0.5 / math.sqrt(HEAD_DIM)
    inside = mask_ref[...] > 0.0
    for head in range(bias_ref.shape[0]):
        cols = slice(head * HEAD_DIM, (head + 1) * HEAD_DIM)
        queries = jnp.concatenate(
            [q_ref[order_ref[i], :, cols] for i in range(len(out_refs))], axis=0
        )
        scores = lax.dot_general(
            queries, k_ref[:, cols], (((1,), (1,)), ((), ())), preferred_element_type=jnp.float32
        )
        half = scores * scale + bias_ref[head]
        weights = jnp.where(inside, half + half * jnp.tanh(half), 0.0).astype(jnp.bfloat16)
        sums = jnp.dot(weights, v_ref[:, cols], preferred_element_type=jnp.float32)
        for i, out_ref in enumerate(out_refs):
            out_ref[:, cols] = sums[i * rows : (i + 1) * rows].astype(out_ref.dtype)


def attend(order, queries, history, bias, mask, per_step):
    blocks, rows, full = queries.shape
    positions = history.shape[0]
    width = per_step * HEAD_DIM
    steps = full // width
    count = order.shape[0]
    return pl.pallas_call(
        attend_kernel,
        grid=(steps,),
        in_specs=[
            pl.BlockSpec(memory_space=pltpu.SMEM),
            pl.BlockSpec((blocks, rows, width), lambda i: (0, 0, i)),
            pl.BlockSpec((positions, width), lambda i: (0, i)),
            pl.BlockSpec((positions, width), lambda i: (0, i + steps)),
            pl.BlockSpec((per_step, 1, positions), lambda i: (i, 0, 0)),
            pl.BlockSpec((1, positions), lambda i: (0, 0)),
        ],
        out_specs=[pl.BlockSpec((rows, width), lambda i: (0, i))] * count,
        out_shape=[jax.ShapeDtypeStruct((rows, full), jnp.bfloat16)] * count,
        compiler_params=pltpu.CompilerParams(vmem_limit_bytes=56 * 1024 * 1024),
        cost_estimate=pl.CostEstimate(
            flops=4 * count * rows * positions * full,
            bytes_accessed=4 * positions * full + 4 * count * rows * full,
            transcendentals=count * rows * positions * full // HEAD_DIM,
        ),
    )(order, queries, history, history, bias, mask)


def attend_whole_kernel(order_ref, q_ref, history_ref, bias_ref, mask_ref, *out_refs):
    rows, width = out_refs[0].shape
    attend_kernel(
        order_ref,
        q_ref,
        history_ref.at[:, :width],
        history_ref.at[:, width:],
        bias_ref,
        mask_ref,
        *out_refs,
    )


def attend_whole(order, queries, history, bias, mask):
    _, rows, full = queries.shape
    positions = history.shape[0]
    count = order.shape[0]
    vmem = pl.BlockSpec(memory_space=pltpu.VMEM)
    return pl.pallas_call(
        attend_whole_kernel,
        in_specs=[pl.BlockSpec(memory_space=pltpu.SMEM)] + [vmem] * 4,
        out_specs=[vmem] * count,
        out_shape=[jax.ShapeDtypeStruct((rows, full), jnp.bfloat16)] * count,
        compiler_params=pltpu.CompilerParams(vmem_limit_bytes=24 * 1024 * 1024),
        cost_estimate=pl.CostEstimate(
            flops=4 * count * rows * positions * full,
            bytes_accessed=4 * positions * full + 4 * count * rows * full,
            transcendentals=count * rows * positions * full // HEAD_DIM,
        ),
    )(order, queries, history, bias, mask)


def own_kernel(q_ref, own_ref, self_bias_ref, out_ref):
    width = q_ref.shape[1]
    scale = 0.5 / math.sqrt(HEAD_DIM)
    for head in range(width // HEAD_DIM):
        cols = slice(head * HEAD_DIM, (head + 1) * HEAD_DIM)
        value_cols = slice(width + head * HEAD_DIM, width + (head + 1) * HEAD_DIM)
        product = q_ref[:, cols].astype(jnp.float32) * own_ref[:, cols].astype(jnp.float32)
        half = jnp.sum(product, axis=-1, keepdims=True) * scale + 0.5 * self_bias_ref[0, head]
        weight = (half + half * jnp.tanh(half)).astype(jnp.bfloat16).astype(jnp.float32)
        out_ref[:, cols] = weight * own_ref[:, value_cols].astype(jnp.float32)


def own_term(queries, own, self_bias):
    rows, width = queries.shape
    block = 32
    return pl.pallas_call(
        own_kernel,
        grid=(rows // block,),
        in_specs=[
            pl.BlockSpec((block, width), lambda i: (i, 0)),
            pl.BlockSpec((block, 2 * width), lambda i: (i, 0)),
            pl.BlockSpec(memory_space=pltpu.SMEM),
        ],
        out_specs=pl.BlockSpec((block, width), lambda i: (i, 0)),
        out_shape=jax.ShapeDtypeStruct((rows, width), jnp.float32),
    )(queries, own, self_bias[None])


def finish_kernel(flag_ref, d_ref, c_ref, b_ref, a_ref, base_ref, gate_ref, gain_ref, out_ref):
    a, b, c, d = (ref[...].astype(jnp.float32) for ref in (a_ref, b_ref, c_ref, d_ref))
    odd, even = a + c, b + d
    even_low = flag_ref[0] == 1
    low = jnp.where(even_low, even, odd)
    high = jnp.where(even_low, odd, even)
    total = base_ref[...] + jnp.concatenate([low, high], axis=-1)
    average = jnp.mean(total, axis=-1, keepdims=True)
    centered = total - average
    variance = jnp.mean(centered * centered, axis=-1, keepdims=True)
    normed = centered * lax.rsqrt(variance + 1e-05) * gain_ref[...]
    out_ref[...] = (normed * gate_ref[...].astype(jnp.float32)).astype(out_ref.dtype)


def finish(flag, parts, base, gate, gain):
    rows, width = gate.shape
    block = 64
    row_spec = lambda cols: pl.BlockSpec((block, cols), lambda i: (i, 0))
    return pl.pallas_call(
        finish_kernel,
        grid=(rows // block,),
        in_specs=[pl.BlockSpec(memory_space=pltpu.SMEM)]
        + [row_spec(width // 2)] * 4
        + [row_spec(width), row_spec(width), pl.BlockSpec((1, width), lambda i: (0, 0))],
        out_specs=row_spec(width),
        out_shape=jax.ShapeDtypeStruct((rows, width), jnp.bfloat16),
        compiler_params=pltpu.CompilerParams(vmem_limit_bytes=12 * 1024 * 1024),
    )(flag[None], *parts[::-1], base, gate, gain[None])


def swapped(value):
    return lax.ppermute(value, "core", [(0, 1), (1, 0)])


def per_device(
    cand_query,
    cand_kv,
    cand_gate,
    cache_store,
    holders,
    lengths,
    buckets,
    time_bias,
    self_bias,
    norm_gain,
):
    core = lax.axis_index("core")
    upper_y = lax.axis_index("yh1")
    side = upper_y ^ lax.axis_index("yh0")
    group_index = lax.axis_index(GROUP)
    groups = lax.axis_size(GROUP)
    z_size = lax.axis_size("z")
    slots, _, piece_len, double_width = cache_store.shape
    width = double_width // 2
    half_width = width // 2

    holding = (holders // slots).reshape(groups, slots)
    slot_of = (holders % slots).reshape(groups, slots)
    chosen = jnp.sum(jnp.where(holding == group_index, slot_of, 0), axis=1).reshape(groups // 2, 2).T
    chosen = jnp.where(upper_y == 0, chosen, chosen[::-1]).reshape(-1)
    picked = cache_store[chosen, 0].reshape(groups, 1, piece_len, double_width)
    outgoing = jnp.concatenate(
        [
            jnp.concatenate(
                [
                    picked[..., h * half_width : (h + 1) * half_width],
                    picked[..., width + h * half_width : width + (h + 1) * half_width],
                ],
                axis=-1,
            )
            for h in range(2)
        ],
        axis=1,
    ).reshape(2 * groups, piece_len, width)
    incoming = lax.all_to_all(outgoing, ("yh0",) + GROUP, 0, 0, tiled=True)
    pieces = incoming.reshape(2 * groups * piece_len, width)
    history = lax.all_gather(pieces, "z", tiled=True)

    queries = cand_query[0]
    own_half = lax.dynamic_slice_in_dim(queries, core * half_width, half_width, 1)
    other_half = lax.dynamic_slice_in_dim(queries, (1 - core) * half_width, half_width, 1)
    partner_half = swapped(other_half)
    first = jnp.where(core == 0, own_half, partner_half)
    second = jnp.where(core == 0, partner_half, own_half)
    spread = lax.all_to_all(jnp.stack([first, second, second, first]), Y, 0, 0, tiled=True)

    about = jnp.concatenate([buckets[0], lengths])
    about = jnp.where(core == side, about, swapped(about))
    session = (group_index // 2) * 2 + side
    own_holding = lax.dynamic_index_in_dim(holding, session, 0, keepdims=False)
    arrived = own_holding[None, :] == jnp.arange(groups, dtype=jnp.int32)[:, None]
    piece_of = jnp.sum(jnp.where(arrived, jnp.arange(slots, dtype=jnp.int32)[None, :], 0), axis=1)
    half_rows = about.shape[0] // 2
    rows = lax.dynamic_slice_in_dim(about[:-1], upper_y * half_rows, half_rows).astype(jnp.float32)
    rows = rows.reshape(2, z_size, slots, piece_len)
    rows = jnp.einsum("sj,yzjr->zysr", arrived.astype(jnp.float32), rows, precision=lax.Precision.HIGHEST)
    rows = rows.reshape(z_size, -1)
    loop = jnp.arange(z_size, dtype=jnp.int32)[:, None, None, None]
    loop = loop + z_size * (2 * upper_y + jnp.arange(2, dtype=jnp.int32)[None, :, None, None])
    place = (loop * slots + piece_of[None, None, :, None]) * piece_len
    place = (place + jnp.arange(piece_len, dtype=jnp.int32)[None, None, None, :]).reshape(z_size, -1)
    own_bias = 0.5 * lax.dynamic_slice_in_dim(time_bias, core * (HEADS // 2), HEADS // 2, 1)

    numbers = rows.reshape(-1, 1)
    table = jnp.arange(time_bias.shape[0], dtype=jnp.int32).astype(jnp.float32)
    one_hot = (jnp.abs(numbers - table[None, :]) < 0.5).astype(jnp.float32)
    bias = jnp.einsum("kn,nh->hk", one_hot, own_bias, precision=lax.Precision.HIGHEST)[:, None, :]
    mask = (place.reshape(1, -1) < about[-1]).astype(jnp.float32)
    base = own_term(queries, cand_kv[0], self_bias)
    order = send_order()[lax.axis_index(Y + ("core",))]
    near_queries = jnp.stack([spread[order[0]], spread[order[1]]])
    bias, mask, base, order = lax.optimization_barrier((bias, mask, base, order))
    far = attend(order[2:], spread, history, bias, mask, PER_STEP)
    *far, rest = lax.optimization_barrier((*far, jnp.arange(2, dtype=jnp.int32)))
    near = attend_whole(rest, near_queries, history, bias, mask)
    partial = [*near, *far]
    parts = [lax.ppermute(partial[s], Y + ("core",), send_pairs(s)) for s in range(4)]
    flag = ((core == 0) == (core == side)).astype(jnp.int32)
    return finish(flag, parts, base, cand_gate[0], norm_gain)[None]


def solution(mesh):
    split = Mesh(mesh.devices.reshape(2, 2, 8, 4, 2, 2), LOOP + GROUP)
    rows = P(GROUP, LOOP, None)
    return jax.shard_map(
        per_device,
        mesh=split,
        in_specs=(
            rows,
            rows,
            rows,
            P(GROUP, LOOP, None, None),
            P(),
            P(GROUP),
            P(GROUP, None),
            P(),
            P(),
            P(),
        ),
        out_specs=rows,
        check_vma=False,
    )
```
